512 devices in a mesh: pts: 64 (over z, x_hi, core), sub: 8 (over x_lo, y).
Axes of the slice: x: 4 (x_hi: 2, x_lo: 2; x = x_hi * 2 + x_lo), y: 4, z: 16, core: 2. Of those that a mesh axis runs over, the one named last changes fastest.
Arguments:
- points: bfloat16 [262144, 256], P(('pts', 'sub')), may hold values from -6 to 6
- counts: int32 [64, 8], P('pts', 'sub'), may hold values from 1 to 512, as said below
- norm_gain: float32 [256], replicated, may hold values from 0.25 to 1.75
- w_fx: bfloat16 [256, 256], replicated, may hold values from -0.375 to 0.375
- w_slice: bfloat16 [256, 512], replicated, may hold values from -0.375 to 0.375
- temper: float32 [8], replicated, may hold values from 0.03 to 0.6
- query_projection: float32 [8, 32, 32], replicated, may hold values from -1 to 1
- key_projection: float32 [8, 32, 32], replicated, may hold values from -1 to 1
- value_projection: float32 [8, 32, 32], replicated, may hold values from -1 to 1
- w_out: bfloat16 [256, 256], replicated, may hold values from -0.375 to 0.375
- cotangent: bfloat16 [262144, 256], P(('pts', 'sub')), may hold values from -6 to 6
Outputs:
- updated: bfloat16 [262144, 256], P(('pts', 'sub'))
- grad_points: bfloat16 [262144, 256], P(('pts', 'sub'))
The draws below stay inside these ranges and needn't reach their ends.
Inputs may be any that keep to these rules, and one draw needn't show every extreme that they name: `counts`: partitions differ in load: a device's count lies near 512, 256 or 128, some device is full.
All inputs are finite; a program needn't handle non-finite values.
Results may differ from the reference program's by a relative error of at most 0.006.
Values sent between devices are 32-bit elements; how exact they have to be, the bound alone decides.
No kernel may reach another device: no remote copies, remote signals or barrier semaphores. Data moves between devices by JAX's collectives and lax.ppermute only.
A program may use at most 64 MiB of HBM per device.

```python
import math
import jax
import jax.numpy as jnp
from jax import lax

D = 256
H = 8
M = 64
DH = 32
ROWS = 512
TOTAL = 262144
N_PTS = 64
N_SUB = 8


def draw_counts(key, part):
    key = jax.random.fold_in(key, 7)
    key_level, key_jitter, key_full = jax.random.split(key, 3)
    level = jax.random.randint(key_level, (N_PTS, 1), 0, 3)
    top = jnp.right_shift(jnp.full((N_PTS, 1), ROWS, jnp.int32), level)
    jitter = jax.random.randint(key_jitter, (N_PTS, N_SUB), 0, top // 4 + 1)
    slice_values = (top - jitter).reshape(-1)
    spot = jax.random.randint(key_full, (), 0, N_PTS * N_SUB)
    slice_values = jnp.where(jnp.arange(N_PTS * N_SUB) == spot, ROWS, slice_values)
    return jnp.maximum(slice_values, 1).reshape(N_PTS, N_SUB).astype(jnp.int32)


def steps_of(stream_key, shape, cuts, smallest, largest):
    loudness = 1.0
    for position, parts in cuts:
        heights = jax.random.uniform(jax.random.fold_in(jax.random.fold_in(stream_key, 6), position), (parts,), jnp.float32, smallest / len(cuts), largest / len(cuts))
        loudness = loudness * jnp.repeat(jnp.exp(heights), shape[position] // parts).reshape((-1,) + (1,) * (len(shape) - 1 - position))
    return loudness


def bell_draw(stream_key, extent, scale, most, cuts=(), kind=jnp.bfloat16):
    values = jax.random.normal(stream_key, extent, jnp.float32) * scale
    if len(cuts) > 0:
        values = steps_of(stream_key, extent, cuts, -0.22, 0.18) * values
    return jnp.clip(values, min=-most, max=most).astype(kind)


def setup_inputs(seed: int = 0) -> dict:
    splits = jax.random.split(jax.random.key(seed), 12)
    return {
        "points": bell_draw(splits[0], (TOTAL, D), 1.0, 6.0, ((0, 512),)),
        "counts": draw_counts(jax.random.fold_in(splits[11], 71), 0),
        "norm_gain": jnp.clip(1.0 + 0.15 * jax.random.normal(splits[2], (D,), jnp.float32), 0.25, 1.75),
        "w_fx": bell_draw(splits[3], (D, D), D ** -0.5, 0.375),
        "w_slice": bell_draw(splits[4], (D, H * M), D ** -0.5, 0.375),
        "temper": jnp.clip(jnp.exp(jax.random.uniform(splits[5], (H,), jnp.float32, math.log(0.03), math.log(0.6))), 0.03, 0.6),
        "query_projection": bell_draw(splits[6], (H, DH, DH), DH ** -0.5, 1.0, (), jnp.float32),
        "key_projection": bell_draw(splits[7], (H, DH, DH), DH ** -0.5, 1.0, (), jnp.float32),
        "value_projection": bell_draw(splits[8], (H, DH, DH), DH ** -0.5, 1.0, (), jnp.float32),
        "w_out": bell_draw(splits[9], (D, D), D ** -0.5, 0.375),
        "cotangent": bell_draw(splits[10], (TOTAL, D), 1.0, 6.0, ((0, 512),)),
    }


def forward_parts(xf, live, norm_gain, w_fx, w_slice, temper):
    rows = xf.shape[0]
    heads = temper.shape[0]
    mean = lax.optimization_barrier(jnp.mean(xf, -1, keepdims=True))
    cent = xf - mean
    var = lax.optimization_barrier(jnp.mean(cent * cent, -1, keepdims=True))
    normed = (cent * lax.rsqrt(var + 1e-05) * norm_gain).astype(jnp.bfloat16)
    point_features = jnp.dot(normed, w_fx, preferred_element_type=jnp.float32).reshape(rows, heads, -1)
    logits = jnp.dot(normed, w_slice, preferred_element_type=jnp.float32).reshape(rows, heads, -1)
    slice_weights = jax.nn.softmax(logits / temper[None, :, None], axis=-1) * live[:, None, None]
    numerator_sum = jnp.einsum('wba,wbz->baz', slice_weights, point_features, precision=lax.Precision.HIGHEST)
    den = lax.optimization_barrier(jnp.sum(slice_weights, axis=0))
    return (numerator_sum, den, slice_weights)

def slice_attention(numerator_sum, den, query_projection, key_projection, value_projection):
    slice_tokens = numerator_sum / (den[..., None] + 1e-05)
    slice_query = jnp.einsum('xlw,xwi->xli', slice_tokens, query_projection, precision=lax.Precision.HIGHEST)
    slice_keys = jnp.einsum('xlw,xwi->xli', slice_tokens, key_projection, precision=lax.Precision.HIGHEST)
    slice_values = jnp.einsum('xlw,xwi->xli', slice_tokens, value_projection, precision=lax.Precision.HIGHEST)
    scores = jnp.einsum('hme,hne->hmn', slice_query, slice_keys, precision=lax.Precision.HIGHEST) / jnp.sqrt(jnp.float32(slice_query.shape[-1]))
    probs = jax.nn.softmax(scores, axis=-1)
    return jnp.einsum('hmn,hne->hme', probs, slice_values, precision=lax.Precision.HIGHEST)

def deslice(xf, slice_weights, att, w_out):
    rows = xf.shape[0]
    mixed = jnp.einsum('rhm,hme->rhe', slice_weights, att, precision=lax.Precision.HIGHEST)
    mixed = mixed.reshape(rows, -1).astype(jnp.bfloat16)
    return xf + jnp.dot(mixed, w_out, preferred_element_type=jnp.float32)

def reference(points, counts, norm_gain, w_fx, w_slice, temper, query_projection, key_projection, value_projection, w_out, cotangent):
    rows = points.shape[0]
    index = jnp.arange(rows, dtype=jnp.int32)
    owner = index // ROWS
    local = index % ROWS
    live = (local < counts.reshape(-1)[owner]).astype(jnp.float32)

    def whole(xf):
        numerator_sum, den, slice_weights = forward_parts(xf, live, norm_gain, w_fx, w_slice, temper)
        att = slice_attention(numerator_sum, den, query_projection, key_projection, value_projection)
        return deslice(xf, slice_weights, att, w_out)
    updated, pull = jax.vjp(whole, points.astype(jnp.float32))
    grad = pull(cotangent.astype(jnp.float32))[0]
    return (updated.astype(jnp.bfloat16), grad.astype(jnp.bfloat16))
```

```python
import jax
import jax.numpy as jnp
from jax import lax
from jax.sharding import Mesh, PartitionSpec as P

PLANE = ("xh", "c", "xl", "y")
ALL = ("z", "xh", "c", "xl", "y")


def forward_parts(xf, live, norm_gain, w_fx, w_slice, temper):
    rows = xf.shape[0]
    heads = temper.shape[0]
    mean = jnp.mean(xf, -1, keepdims=True)
    cent = xf - mean
    var = jnp.mean(cent * cent, -1, keepdims=True)
    normed = (cent * lax.rsqrt(var + 1e-05) * norm_gain).astype(jnp.bfloat16)
    point_features = jnp.dot(normed, w_fx, preferred_element_type=jnp.float32).reshape(
        rows, heads, -1
    )
    logits = jnp.dot(normed, w_slice, preferred_element_type=jnp.float32).reshape(rows, heads, -1)
    slice_weights = jax.nn.softmax(logits / temper[None, :, None], axis=-1) * live[:, None, None]
    numerator_sum = jnp.einsum(
        "wba,wbz->baz", slice_weights, point_features, precision=lax.Precision.HIGHEST
    )
    den = jnp.sum(slice_weights, axis=0)
    return (numerator_sum, den, slice_weights)


def slice_attention(numerator_sum, den, query_projection, key_projection, value_projection):
    slice_tokens = numerator_sum / (den[..., None] + 1e-05)
    slice_query = jnp.einsum(
        "xlw,xwi->xli", slice_tokens, query_projection, precision=lax.Precision.HIGHEST
    )
    slice_keys = jnp.einsum(
        "xlw,xwi->xli", slice_tokens, key_projection, precision=lax.Precision.HIGHEST
    )
    slice_values = jnp.einsum(
        "xlw,xwi->xli", slice_tokens, value_projection, precision=lax.Precision.HIGHEST
    )
    scores = jnp.einsum(
        "hme,hne->hmn", slice_query, slice_keys, precision=lax.Precision.HIGHEST
    ) / jnp.sqrt(jnp.float32(slice_query.shape[-1]))
    probs = jax.nn.softmax(scores, axis=-1)
    return jnp.einsum("hmn,hne->hme", probs, slice_values, precision=lax.Precision.HIGHEST)


def deslice(xf, slice_weights, att, w_out):
    rows = xf.shape[0]
    mixed = jnp.einsum("rhm,hme->rhe", slice_weights, att, precision=lax.Precision.HIGHEST)
    mixed = mixed.reshape(rows, -1).astype(jnp.bfloat16)
    return xf + jnp.dot(mixed, w_out, preferred_element_type=jnp.float32)


def sum_all(flat):
    part = lax.all_to_all(flat.reshape(32, 9, 1, 128), PLANE, 0, 0).sum(0)
    part = lax.all_to_all(jnp.broadcast_to(part[None], (16, 9, 1, 128)), "z", 0, 0).sum(0)
    whole = lax.all_to_all(jnp.broadcast_to(part[None], (32, 9, 1, 128)), PLANE, 0, 0)
    return whole.reshape(288, 128)


def per_device(
    points,
    counts,
    norm_gain,
    w_fx,
    w_slice,
    temper,
    query_projection,
    key_projection,
    value_projection,
    w_out,
    cotangent,
):
    rows = points.shape[0]
    live = (jnp.arange(rows, dtype=jnp.int32) < counts[0, 0]).astype(jnp.float32)
    xf = points.astype(jnp.float32)

    def front(xv):
        return forward_parts(xv, live, norm_gain, w_fx, w_slice, temper)

    (num_part, den_part, slice_weights), pull_front = jax.vjp(front, xf)

    def back(xv, weights_in, att_in):
        return deslice(xv, weights_in, att_in, w_out)

    gmixed = jnp.dot(cotangent, w_out.T, preferred_element_type=jnp.float32).astype(jnp.bfloat16)
    gatt_part = jnp.einsum(
        "rhm,rhe->hme",
        slice_weights,
        gmixed.astype(jnp.float32).reshape(rows, 8, 32),
        precision=lax.Precision.HIGHEST,
    )
    flat = jnp.concatenate(
        [
            num_part.reshape(128, 128),
            gatt_part.reshape(128, 128),
            den_part.reshape(4, 128),
            jnp.zeros((28, 128), jnp.float32),
        ]
    )
    flat = sum_all(flat)
    numerator_sum = flat[:128].reshape(8, 64, 32)
    grad_att = flat[128:256].reshape(8, 64, 32)
    den = flat[256:260].reshape(8, 64)

    def middle(num_in, den_in):
        return slice_attention(num_in, den_in, query_projection, key_projection, value_projection)

    att, pull_middle = jax.vjp(middle, numerator_sum, den)
    updated, pull_back = jax.vjp(back, xf, slice_weights, att)
    grad_direct, grad_weights, _ = pull_back(cotangent.astype(jnp.float32))
    grad_num, grad_den = pull_middle(grad_att)
    grad_front = pull_front((grad_num, grad_den, grad_weights))[0]
    grad = (grad_direct + grad_front).astype(jnp.bfloat16)
    return (updated.astype(jnp.bfloat16), grad)


def solution(mesh):
    fine = Mesh(mesh.devices.reshape(16, 2, 2, 2, 4), ALL)
    rows = P(ALL, None)
    return jax.shard_map(
        per_device,
        mesh=fine,
        in_specs=(rows, P(("z", "xh", "c"), ("xl", "y"))) + (P(),) * 8 + (rows,),
        out_specs=(rows, rows),
        check_vma=False,
    )
```

```python
import math

import jax
import jax.numpy as jnp
from jax import lax
from jax.experimental import pallas as pl
from jax.experimental.pallas import tpu as pltpu
from jax.sharding import Mesh, PartitionSpec as P

PLANE = ("xh", "c", "xl", "y")
ALL = ("z", "xh", "c", "xl", "y")
HEADS, SLICES, DH = 8, 64, 32
F32, BF16 = jnp.float32, jnp.bfloat16


def dot(a, b, ca, cb, precision=None):
    return lax.dot_general(
        a, b, (((ca,), (cb,)), ((), ())), precision=precision, preferred_element_type=F32
    )


def exact(a, b, ca, cb):
    return dot(a, b, ca, cb, lax.Precision.HIGHEST)


def normalise(x):
    cent = x - jnp.mean(x, -1, keepdims=True)
    rstd = lax.rsqrt(jnp.mean(cent * cent, -1, keepdims=True) + 1e-05)
    return cent * rstd, rstd


def front_kernel(
    count, temper, x_ref, gain, w_fx, w_slice, w_out, cot, flat, w_t, c_t, logit_t, w_bf
):
    rows = x_ref.shape[0]
    normed = (normalise(x_ref[...].astype(F32))[0] * gain[...]).astype(BF16)
    logit_t[...] = dot(w_slice[...].T, normed, 1, 1)
    feats = dot(w_fx[...].T, normed, 1, 1).astype(BF16)
    gmix = dot(w_out[...], cot[...], 1, 1).astype(BF16)
    for h in range(HEADS):
        c_t[h * 64 : h * 64 + 32, :] = feats[h * 32 : h * 32 + 32, :]
        c_t[h * 64 + 32 : h * 64 + 64, :] = gmix[h * 32 : h * 32 + 32, :]
    live = (lax.broadcasted_iota(jnp.int32, (1, rows), 1) < count[0, 0]).astype(F32)
    for h in range(HEADS):
        part = slice(h * SLICES, (h + 1) * SLICES)
        logits = logit_t[part, :]
        scale = 1.0 / jnp.full((1, rows), temper[h], F32)
        e = jnp.exp((logits - jnp.max(logits, 0, keepdims=True)) * scale)
        w = e * (live / jnp.sum(e, 0, keepdims=True))
        w_t[part, :] = w
        w_bf[part, :] = w.astype(BF16)
    lane = lax.broadcasted_iota(jnp.int32, (64, 128), 1)
    for p in range(4):
        part = slice(p * 128, (p + 1) * 128)
        both = dot(w_bf[part, :], c_t[part, :], 1, 1)
        flat[p * 64 : (p + 1) * 64, :] = jnp.where(lane < 64, both[:64], both[64:])
    den = dot(jnp.ones((8, rows), BF16), w_bf[...], 1, 1)
    flat[256:288, :] = jnp.zeros((32, 128), F32)
    for p in range(4):
        flat[256 + p : 257 + p, :] = den[0:1, p * 128 : (p + 1) * 128]


def middle(flat, query, key, value, b_hi, b_lo, gden):
    den_cols = flat[256:264, :].T
    own = (
        lax.broadcasted_iota(jnp.int32, (128, 128), 0) // 64
        == lax.broadcasted_iota(jnp.int32, (128, 128), 1) // 64
    )
    for p in range(4):
        heads = (2 * p, 2 * p + 1)
        t = flat[p * 64 : (p + 1) * 64, :]
        rec = 1.0 / (den_cols[:, p : p + 1] + 1e-05)
        tok = jnp.concatenate([t[:, 0:32], t[:, 64:96]], 0) * rec
        g_att = jnp.concatenate([t[:, 32:64], t[:, 96:128]], 0)

        def project(a, weights, side):
            return jnp.concatenate(
                [exact(a[i * 64 : (i + 1) * 64], weights[h], 1, side) for i, h in enumerate(heads)],
                0,
            )

        q, k, v = project(tok, query, 0), project(tok, key, 0), project(tok, value, 0)
        scale = 1.0 / math.sqrt(DH)
        s = jnp.where(own, exact(q, k, 1, 1) * scale, -jnp.inf)
        e = jnp.exp(s - jnp.max(s, -1, keepdims=True))
        prob = e / jnp.sum(e, -1, keepdims=True)
        att = exact(prob, v, 1, 0)
        g_v = exact(prob, g_att, 0, 0)
        g_prob = exact(g_att, v, 1, 1)
        g_s = prob * (g_prob - jnp.sum(prob * g_prob, -1, keepdims=True)) * scale
        g_q, g_k = exact(g_s, k, 1, 0), exact(g_s, q, 0, 0)
        g_tok = project(g_q, query, 1) + project(g_k, key, 1) + project(g_v, value, 1)
        g_num = g_tok * rec
        gden[p * 128 : (p + 1) * 128, :] = -jnp.sum(tok * g_num, -1, keepdims=True)
        block = jnp.concatenate([g_num, att], 1)
        block = jnp.where(own, jnp.concatenate([block, block], 1), 0.0)
        hi = block.astype(BF16)
        b_hi[p * 128 : (p + 1) * 128, :] = hi
        b_lo[p * 128 : (p + 1) * 128, :] = (block - hi.astype(F32)).astype(BF16)


def back_kernel(
    temper, flat, query, key, value, x_ref, gain, w_fx, w_slice, w_out, cot, w_t, c_t,
    updated, grad, b_hi, b_lo, gden, g_logit, g_feat, mixed_t,
):
    rows = x_ref.shape[0]
    middle(flat, query, key, value, b_hi, b_lo, gden)
    for p in range(4):
        part = slice(p * 128, (p + 1) * 128)
        w = w_t[part, :]
        both = dot(b_hi[part, :], w.astype(BF16), 0, 0)
        c = c_t[part, :]
        g_w = dot(b_hi[part, :], c, 1, 0) + dot(b_lo[part, :], c, 1, 0) + gden[part, :]
        for i in range(2):
            h = 2 * p + i
            g_feat[h * 32 : (h + 1) * 32, :] = both[i * 64 : i * 64 + 32].astype(BF16)
            mixed_t[h * 32 : (h + 1) * 32, :] = both[i * 64 + 32 : i * 64 + 64]
            mine = slice(i * 64, (i + 1) * 64)
            scale = 1.0 / jnp.full((1, rows), temper[h], F32)
            wh, gh = w[mine], g_w[mine]
            mean = jnp.sum(wh * gh, 0, keepdims=True)
            g_logit[h * 64 : (h + 1) * 64, :] = (wh * (gh - mean) * scale).astype(BF16)
    x = x_ref[...].astype(F32)
    mixed = mixed_t[...].T.astype(BF16)
    updated[...] = (x + dot(mixed, w_out[...], 1, 0)).astype(BF16)
    g_normed = dot(w_slice[...], g_logit[...], 1, 0) + dot(w_fx[...], g_feat[...], 1, 0)
    g_normed = g_normed.T.astype(BF16).astype(F32)
    xhat, rstd = normalise(x)
    g_hat = g_normed * gain[...]
    along = jnp.mean(g_hat * xhat, -1, keepdims=True)
    g_x = rstd * (g_hat - jnp.mean(g_hat, -1, keepdims=True) - xhat * along)
    grad[...] = (cot[...].astype(F32) + g_x).astype(BF16)


def sum_all(flat):
    part = lax.all_to_all(flat.reshape(32, 9, 1, 128), PLANE, 0, 0).sum(0)
    part = lax.all_to_all(jnp.broadcast_to(part[None], (16, 9, 1, 128)), "z", 0, 0).sum(0)
    whole = lax.all_to_all(jnp.broadcast_to(part[None], (32, 9, 1, 128)), PLANE, 0, 0)
    return whole.reshape(288, 128)


VMEM = pl.BlockSpec(memory_space=pltpu.VMEM)
SMEM = pl.BlockSpec(memory_space=pltpu.SMEM)
PARAMS = pltpu.CompilerParams(vmem_limit_bytes=32 * 1024 * 1024)


def per_device(
    points,
    counts,
    norm_gain,
    w_fx,
    w_slice,
    temper,
    query_projection,
    key_projection,
    value_projection,
    w_out,
    cotangent,
):
    rows, width = points.shape
    gain = norm_gain.reshape(1, width)
    n = HEADS * SLICES
    flat, w_t, c_t = pl.pallas_call(
        front_kernel,
        out_shape=(
            jax.ShapeDtypeStruct((288, 128), F32),
            jax.ShapeDtypeStruct((n, rows), F32),
            jax.ShapeDtypeStruct((n, rows), BF16),
        ),
        in_specs=[SMEM] * 2 + [VMEM] * 6,
        out_specs=(VMEM,) * 3,
        scratch_shapes=[pltpu.VMEM((n, rows), F32), pltpu.VMEM((n, rows), BF16)],
        compiler_params=PARAMS,
        name="front",
    )(counts, temper, points, gain, w_fx, w_slice, w_out, cotangent)
    flat = sum_all(flat)
    return pl.pallas_call(
        back_kernel,
        out_shape=(jax.ShapeDtypeStruct((rows, width), BF16),) * 2,
        in_specs=[SMEM] + [VMEM] * 12,
        out_specs=(VMEM,) * 2,
        scratch_shapes=[
            pltpu.VMEM((n, 128), BF16),
            pltpu.VMEM((n, 128), BF16),
            pltpu.VMEM((n, 1), F32),
            pltpu.VMEM((n, rows), BF16),
            pltpu.VMEM((width, rows), BF16),
            pltpu.VMEM((width, rows), F32),
        ],
        compiler_params=PARAMS,
        name="back",
    )(
        temper, flat, query_projection, key_projection, value_projection, points, gain, w_fx,
        w_slice, w_out, cotangent, w_t, c_t,
    )


def solution(mesh):
    fine = Mesh(mesh.devices.reshape(16, 2, 2, 2, 4), ALL)
    rows = P(ALL, None)
    return jax.shard_map(
        per_device,
        mesh=fine,
        in_specs=(rows, P(("z", "xh", "c"), ("xl", "y"))) + (P(),) * 8 + (rows,),
        out_specs=(rows, rows),
        check_vma=False,
    )
```

```python
import math

import jax
import jax.numpy as jnp
from jax import lax
from jax.experimental import pallas as pl
from jax.experimental.pallas import tpu as pltpu
from jax.sharding import Mesh, PartitionSpec as P

PLANE = ("xh", "c", "xl", "y")
ALL = ("z", "xh", "c", "xl", "y")
HEADS, SLICES, DH = 8, 64, 32
F32, BF16 = jnp.float32, jnp.bfloat16


def dot(a, b, ca, cb, precision=None):
    return lax.dot_general(
        a, b, (((ca,), (cb,)), ((), ())), precision=precision, preferred_element_type=F32
    )


def exact(a, b, ca, cb):
    a_hi, b_hi = a.astype(BF16), b.astype(BF16)
    a_lo, b_lo = (a - a_hi.astype(F32)).astype(BF16), (b - b_hi.astype(F32)).astype(BF16)
    return dot(a_hi, b_hi, ca, cb) + (dot(a_lo, b_hi, ca, cb) + dot(a_hi, b_lo, ca, cb))


def normalise(x):
    cent = x - jnp.mean(x, -1, keepdims=True)
    rstd = lax.rsqrt(jnp.mean(cent * cent, -1, keepdims=True) + 1e-05)
    return cent * rstd, rstd


def front_kernel(*refs):
    count, temper_hbm = refs[:2]
    sources = refs[2:11]
    flat, w_t, c_t, scales = refs[11:15]
    targets = refs[15:24]
    temper, logit_t, w_bf, sems = refs[24:]
    x_ref, gain, w_slice, w_fx, w_out, cot = targets[:6]
    rows = x_ref.shape[0]
    copies = [
        pltpu.make_async_copy(a, b, sems.at[i])
        for i, (a, b) in enumerate(zip((*sources, temper_hbm), (*targets, temper)))
    ]
    for copy in copies:
        copy.start()
    copies[0].wait()
    copies[1].wait()
    normed = (normalise(x_ref[...].astype(F32))[0] * gain[...]).astype(BF16)
    for copy in copies[2:]:
        copy.wait()
    logit_t[...] = dot(w_slice[...].T, normed, 1, 1)
    feats = dot(w_fx[...].T, normed, 1, 1).astype(BF16)
    gmix = dot(w_out[...], cot[...], 1, 1).astype(BF16)
    for h in range(HEADS):
        c_t[h * 64 : h * 64 + 32, :] = feats[h * 32 : h * 32 + 32, :]
        c_t[h * 64 + 32 : h * 64 + 64, :] = gmix[h * 32 : h * 32 + 32, :]
    live = (lax.broadcasted_iota(jnp.int32, (1, rows), 1) < count[0, 0]).astype(F32)
    for h in range(HEADS):
        part = slice(h * SLICES, (h + 1) * SLICES)
        logits = logit_t[part, :]
        scale = 1.0 / jnp.full((1, rows), temper[h], F32)
        scales[h : h + 1, :] = scale
        e = jnp.exp((logits - jnp.max(logits, 0, keepdims=True)) * scale)
        w = e * (live / jnp.sum(e, 0, keepdims=True))
        w_t[part, :] = w
        w_bf[part, :] = w.astype(BF16)
    lane = lax.broadcasted_iota(jnp.int32, (64, 128), 1)
    for p in range(4):
        part = slice(p * 128, (p + 1) * 128)
        both = dot(w_bf[part, :], c_t[part, :], 1, 1)
        flat[p * 64 : (p + 1) * 64, :] = jnp.where(lane < 64, both[:64], both[64:])
    den = dot(jnp.ones((8, rows), BF16), w_bf[...], 1, 1)
    flat[256:288, :] = jnp.zeros((32, 128), F32)
    for p in range(4):
        flat[256 + p : 257 + p, :] = den[0:1, p * 128 : (p + 1) * 128]


def middle(flat, query, key, value, b_hi, b_lo, gden):
    den_cols = flat[256:264, :].T
    own = (
        lax.broadcasted_iota(jnp.int32, (128, 128), 0) // 64
        == lax.broadcasted_iota(jnp.int32, (128, 128), 1) // 64
    )
    pairs = range(4)
    scale = 1.0 / math.sqrt(DH)

    def project(a, weights, side):
        return [
            jnp.concatenate(
                [exact(a[p][i * 64 : (i + 1) * 64], weights[2 * p + i], 1, side) for i in range(2)],
                0,
            )
            for p in pairs
        ]

    def each(f, *lists):
        return [f(*items) for items in zip(*lists)]

    t = [flat[p * 64 : (p + 1) * 64, :] for p in pairs]
    rec = [1.0 / (den_cols[:, p : p + 1] + 1e-05) for p in pairs]
    tok = each(lambda t, r: jnp.concatenate([t[:, 0:32], t[:, 64:96]], 0) * r, t, rec)
    g_att = each(lambda t: jnp.concatenate([t[:, 32:64], t[:, 96:128]], 0), t)
    q, k, v = project(tok, query, 0), project(tok, key, 0), project(tok, value, 0)
    s = each(lambda q, k: jnp.where(own, exact(q, k, 1, 1) * scale, -jnp.inf), q, k)
    g_prob = each(lambda g, v: exact(g, v, 1, 1), g_att, v)
    e = each(lambda s: jnp.exp(s - jnp.max(s, -1, keepdims=True)), s)
    prob = each(lambda e: e / jnp.sum(e, -1, keepdims=True), e)
    g_s = each(
        lambda w, g: w * (g - jnp.sum(w * g, -1, keepdims=True)) * scale, prob, g_prob
    )
    att = each(lambda w, v: exact(w, v, 1, 0), prob, v)
    g_v = each(lambda w, g: exact(w, g, 0, 0), prob, g_att)
    g_q = each(lambda g, k: exact(g, k, 1, 0), g_s, k)
    g_k = each(lambda g, q: exact(g, q, 0, 0), g_s, q)
    g_tok = each(
        lambda a, b, c: a + b + c, project(g_q, query, 1), project(g_k, key, 1), project(g_v, value, 1)
    )
    for p in pairs:
        g_num = g_tok[p] * rec[p]
        gden[p * 128 : (p + 1) * 128, :] = -jnp.sum(tok[p] * g_num, -1, keepdims=True)
        block = jnp.concatenate([g_num, att[p]], 1)
        block = jnp.where(own, jnp.concatenate([block, block], 1), 0.0)
        hi = block.astype(BF16)
        b_hi[p * 128 : (p + 1) * 128, :] = hi
        b_lo[p * 128 : (p + 1) * 128, :] = (block - hi.astype(F32)).astype(BF16)


def back_kernel(
    flat, w_t, c_t, scales, x_ref, gain, w_slice, w_fx, w_out, cot, query, key, value,
    updated, grad, b_hi, b_lo, gden, g_logit, g_feat, mixed_t,
):
    middle(flat, query, key, value, b_hi, b_lo, gden)
    for p in range(4):
        part = slice(p * 128, (p + 1) * 128)
        w = w_t[part, :]
        both = dot(b_hi[part, :], w.astype(BF16), 0, 0)
        c = c_t[part, :]
        g_w = dot(b_hi[part, :], c, 1, 0) + dot(b_lo[part, :], c, 1, 0) + gden[part, :]
        for i in range(2):
            h = 2 * p + i
            g_feat[h * 32 : (h + 1) * 32, :] = both[i * 64 : i * 64 + 32].astype(BF16)
            mixed_t[h * 32 : (h + 1) * 32, :] = both[i * 64 + 32 : i * 64 + 64]
            mine = slice(i * 64, (i + 1) * 64)
            scale = scales[h : h + 1, :]
            wh, gh = w[mine], g_w[mine]
            mean = jnp.sum(wh * gh, 0, keepdims=True)
            g_logit[h * 64 : (h + 1) * 64, :] = (wh * (gh - mean) * scale).astype(BF16)
    x = x_ref[...].astype(F32)
    mixed = mixed_t[...].T.astype(BF16)
    updated[...] = (x + dot(mixed, w_out[...], 1, 0)).astype(BF16)
    g_normed = dot(w_slice[...], g_logit[...], 1, 0) + dot(w_fx[...], g_feat[...], 1, 0)
    g_normed = g_normed.T.astype(BF16).astype(F32)
    xhat, rstd = normalise(x)
    g_hat = g_normed * gain[...]
    along = jnp.mean(g_hat * xhat, -1, keepdims=True)
    g_x = rstd * (g_hat - jnp.mean(g_hat, -1, keepdims=True) - xhat * along)
    grad[...] = (cot[...].astype(F32) + g_x).astype(BF16)


def sum_all(flat):
    part = lax.all_to_all(flat.reshape(32, 9, 1, 128), PLANE, 0, 0).sum(0)
    part = lax.all_to_all(jnp.broadcast_to(part[None], (16, 9, 1, 128)), "z", 0, 0).sum(0)
    whole = lax.all_to_all(jnp.broadcast_to(part[None], (32, 9, 1, 128)), PLANE, 0, 0)
    return whole.reshape(288, 128)


VMEM = pl.BlockSpec(memory_space=pltpu.VMEM)
SMEM = pl.BlockSpec(memory_space=pltpu.SMEM)
HBM = pl.BlockSpec(memory_space=pltpu.HBM)
PARAMS = pltpu.CompilerParams(vmem_limit_bytes=32 * 1024 * 1024)


def per_device(
    points,
    counts,
    norm_gain,
    w_fx,
    w_slice,
    temper,
    query_projection,
    key_projection,
    value_projection,
    w_out,
    cotangent,
):
    rows, width = points.shape
    gain = norm_gain.reshape(1, width)
    n = HEADS * SLICES
    kept = (
        points, gain, w_slice, w_fx, w_out, cotangent, query_projection, key_projection,
        value_projection,
    )
    flat, *rest = pl.pallas_call(
        front_kernel,
        out_shape=(
            jax.ShapeDtypeStruct((288, 128), F32),
            jax.ShapeDtypeStruct((n, rows), F32),
            jax.ShapeDtypeStruct((n, rows), BF16),
            jax.ShapeDtypeStruct((HEADS, rows), F32),
            *(jax.ShapeDtypeStruct(a.shape, a.dtype) for a in kept),
        ),
        in_specs=[SMEM] + [HBM] * 10,
        out_specs=(VMEM,) * 13,
        scratch_shapes=[
            pltpu.SMEM((HEADS,), F32),
            pltpu.VMEM((n, rows), F32),
            pltpu.VMEM((n, rows), BF16),
            pltpu.SemaphoreType.DMA((10,)),
        ],
        compiler_params=PARAMS,
        name="front",
    )(counts, *(pltpu.with_memory_space_constraint(a, pltpu.HBM) for a in (temper, *kept)))
    return pl.pallas_call(
        back_kernel,
        out_shape=(jax.ShapeDtypeStruct((rows, width), BF16),) * 2,
        in_specs=[VMEM] * 13,
        out_specs=(VMEM,) * 2,
        scratch_shapes=[
            pltpu.VMEM((n, 128), BF16),
            pltpu.VMEM((n, 128), BF16),
            pltpu.VMEM((n, 1), F32),
            pltpu.VMEM((n, rows), BF16),
            pltpu.VMEM((width, rows), BF16),
            pltpu.VMEM((width, rows), F32),
        ],
        compiler_params=PARAMS,
        name="back",
    )(sum_all(flat), *rest)


def solution(mesh):
    fine = Mesh(mesh.devices.reshape(16, 2, 2, 2, 4), ALL)
    rows = P(ALL, None)
    return jax.shard_map(
        per_device,
        mesh=fine,
        in_specs=(rows, P(("z", "xh", "c"), ("xl", "y"))) + (P(),) * 8 + (rows,),
        out_specs=(rows, rows),
        check_vma=False,
    )
```

```python
import math

import jax
import jax.numpy as jnp
from jax import lax
from jax.experimental import pallas as pl
from jax.experimental.pallas import tpu as pltpu
from jax.sharding import Mesh, PartitionSpec as P

PLANE = ("xh", "c", "xl", "y")
ALL = ("z", "xh", "c", "xl", "y")
HEADS, SLICES, DH = 8, 64, 32
F32, BF16 = jnp.float32, jnp.bfloat16


def dot(a, b, ca, cb, precision=None):
    return lax.dot_general(
        a, b, (((ca,), (cb,)), ((), ())), precision=precision, preferred_element_type=F32
    )


def parts(a):
    hi = a.astype(BF16)
    return hi, (a - hi.astype(F32)).astype(BF16)


def dot3(a, b, ca, cb):
    n = b[0].shape[1 - cb]
    left = jnp.concatenate(a, ca)
    right = jnp.concatenate([jnp.concatenate([b[0], b[0]], cb), jnp.concatenate([b[1], jnp.zeros_like(b[1])], cb)], 1 - cb)
    both = dot(left, right, ca, cb)
    return both[:, :n] + both[:, n:]


def normalise(x):
    cent = x - jnp.mean(x, -1, keepdims=True)
    rstd = lax.rsqrt(jnp.mean(cent * cent, -1, keepdims=True) + 1e-05)
    return cent * rstd, rstd


def front_kernel(*refs):
    count, temper_hbm = refs[:2]
    sources = refs[2:11]
    flat, w_t, w_bf, c_t, scales, w_hi, w_lo = refs[11:18]
    temper, logit_t, sems = refs[27:30]
    targets = refs[18:24] + refs[24:27]
    x_ref, gain, w_slice, w_fx, w_out, cot = targets[:6]
    rows = x_ref.shape[0]
    copies = [
        pltpu.make_async_copy(a, b, sems.at[i])
        for i, (a, b) in enumerate(zip((*sources, temper_hbm), (*targets, temper)))
    ]
    for copy in copies:
        copy.start()
    copies[0].wait()
    copies[1].wait()
    normed = (normalise(x_ref[...].astype(F32))[0] * gain[...]).astype(BF16)
    for copy in copies[2:]:
        copy.wait()
    logit_t[...] = dot(w_slice[...].T, normed, 1, 1)
    stack_weights(*targets[6:], w_hi, w_lo)
    feats = dot(w_fx[...].T, normed, 1, 1).astype(BF16)
    gmix = dot(w_out[...], cot[...], 1, 1).astype(BF16)
    for h in range(HEADS):
        c_t[h * 64 : h * 64 + 32, :] = feats[h * 32 : h * 32 + 32, :]
        c_t[h * 64 + 32 : h * 64 + 64, :] = gmix[h * 32 : h * 32 + 32, :]
    live = (lax.broadcasted_iota(jnp.int32, (1, rows), 1) < count[...]).astype(F32)
    for h in range(HEADS):
        part = slice(h * SLICES, (h + 1) * SLICES)
        logits = logit_t[part, :]
        scale = 1.0 / jnp.full((1, rows), temper[h], F32)
        scales[h : h + 1, :] = scale
        e = jnp.exp((logits - jnp.max(logits, 0, keepdims=True)) * scale)
        w = e * (live / jnp.sum(e, 0, keepdims=True))
        w_t[part, :] = w
        w_bf[part, :] = w.astype(BF16)
    lane = lax.broadcasted_iota(jnp.int32, (64, 128), 1)
    for p in range(4):
        part = slice(p * 128, (p + 1) * 128)
        both = dot(w_bf[part, :], c_t[part, :], 1, 1)
        flat[p * 64 : (p + 1) * 64, :] = jnp.where(lane < 64, both[:64], both[64:])
    den = dot(jnp.ones((8, rows), BF16), w_bf[...], 1, 1)
    flat[256:288, :] = jnp.zeros((32, 128), F32)
    for p in range(4):
        flat[256 + p : 257 + p, :] = den[0:1, p * 128 : (p + 1) * 128]


def stack_weights(query, key, value, hi, lo):
    for h in range(HEADS):
        q, k, v = query[h], key[h], value[h]
        a, a_t, v_t = dot3(parts(q), parts(k), 1, 1), dot3(parts(k), parts(q), 1, 1), v.T
        none, gap = jnp.zeros((32, 32), F32), jnp.zeros((32, 64), F32)

        def at(left, right):
            block = jnp.concatenate([left, right], 1)
            return [block, gap] if h % 2 == 0 else [gap, block]

        upper = jnp.concatenate([*at(a, v), *at(a_t, none), gap, gap], 1)
        lower = jnp.concatenate([gap, gap, gap, gap, *at(v_t, none)], 1)
        whole = jnp.concatenate([upper, lower], 0)
        for ref, part in zip((hi, lo), parts(whole)):
            ref[h * 64 : (h + 1) * 64, :] = part


def middle(flat, w_hi, w_lo):
    row = lax.broadcasted_iota(jnp.int32, (128, 128), 0)
    lane = lax.broadcasted_iota(jnp.int32, (128, 128), 1)
    own = row // 64 == lane // 64
    second = (lane // 32) % 2 == 1
    scale = 1.0 / math.sqrt(DH)
    pairs = range(4)

    def each(f, *lists):
        return [f(*items) for items in zip(*lists)]

    def part(p):
        return slice(p * 128, (p + 1) * 128)

    t = [flat[p * 64 : (p + 1) * 64, :] for p in pairs]
    t = each(lambda t: jnp.where(own, jnp.concatenate([t, t], 0), 0.0), t)
    num = each(lambda t: jnp.where(second, 0.0, t), t)
    rec = 1.0 / (flat[256:264, :] + 1e-05)
    along = [rec[p : p + 1, :] for p in pairs]
    rec = rec.T
    down = [rec[:, p : p + 1] for p in pairs]
    split = each(parts, t)
    raw = [dot3(split[p], (w_hi[part(p), :], w_lo[part(p), :]), 1, 0) for p in pairs]
    u_v, u_t, g_v = (each(lambda a: parts(a[:, part(i)]), raw) for i in range(3))
    num_split = each(parts, num)
    s = each(
        lambda u, n, a, d: jnp.where(own, dot3(u, n, 1, 1) * (scale * a) * d, -jnp.inf),
        u_v, num_split, along, down,
    )
    g_prob = each(lambda g, n, a: dot3(g, n, 1, 1) * a, g_v, num_split, along)
    e = each(lambda s: jnp.exp(s - jnp.max(s, -1, keepdims=True)), s)
    prob = each(lambda e: e * (1.0 / jnp.sum(e, -1, keepdims=True)), e)
    g_s = each(lambda w, g: w * (g - jnp.sum(w * g, -1, keepdims=True)) * scale, prob, g_prob)
    g_tok = each(
        lambda g, w, u_v, u_t, g_v, a, d: dot3(parts(g * a), u_t, 1, 0)
        + dot3(parts(g * d), u_v, 0, 0)
        + dot3(parts(w), g_v, 0, 0),
        g_s, prob, u_v, u_t, g_v, along, down,
    )
    att = each(lambda w, a, v: dot3(parts(w * a), v, 1, 0), prob, along, u_v)
    blocks = each(lambda a, g, d: jnp.where(second, a, g * d), att, g_tok, down)
    g_den = each(lambda n, b, d: -jnp.sum(n * b, -1, keepdims=True) * d, num, blocks, down)
    return blocks, g_den


def back_kernel(
    flat, w_t, w_bf, c_t, scales, x_ref, gain, w_slice, w_fx, w_out, cot, w_hi, w_lo,
    updated_hbm, grad_hbm, updated, grad, g_logit, g_feat, mixed_t, sems,
):
    blocks, g_den = middle(flat, w_hi, w_lo)
    split = [parts(b) for b in blocks]
    total, width = x_ref.shape
    half = total // 2
    copies = []

    def leave(i, at, source, target):
        copies.append(pltpu.make_async_copy(source.at[at], target.at[at], sems.at[i]))
        copies[-1].start()

    for j in range(2):
        at = slice(j * half, (j + 1) * half)
        for p in range(4):
            part = slice(p * 128, (p + 1) * 128)
            c = c_t[part, at]
            g_w = dot(jnp.concatenate(split[p], 1), jnp.concatenate([c, c], 0), 1, 0) + g_den[p]
            both = dot(split[p][0], w_bf[part, at], 0, 0)
            for i in range(2):
                h = 2 * p + i
                mine = slice(h * SLICES, (h + 1) * SLICES)
                w, g = w_t[mine, at], g_w[i * 64 : (i + 1) * 64]
                mean = jnp.sum(w * g, 0, keepdims=True)
                g_logit[mine, at] = (w * (g - mean) * scales[h : h + 1, at]).astype(BF16)
                g_feat[h * 32 : (h + 1) * 32, at] = both[i * 64 : i * 64 + 32].astype(BF16)
                mixed_t[h * 32 : (h + 1) * 32, at] = both[i * 64 + 32 : i * 64 + 64]
        x = x_ref[at, :].astype(F32)
        mixed = mixed_t[:, at].T.astype(BF16)
        updated[at, :] = (x + dot(mixed, w_out[...], 1, 0)).astype(BF16)
        leave(2 * j, pl.ds(j * half, half), updated, updated_hbm)
        g_normed = dot(w_slice[...], g_logit[:, at], 1, 0) + dot(w_fx[...], g_feat[:, at], 1, 0)
        g_normed = g_normed.T.astype(BF16).astype(F32)
        hat, rstd = normalise(x)
        g_hat = g_normed * gain[...]
        along = jnp.mean(g_hat * hat, -1, keepdims=True)
        g_x = rstd * (g_hat - jnp.mean(g_hat, -1, keepdims=True) - hat * along)
        grad[at, :] = (cot[at, :].astype(F32) + g_x).astype(BF16)
        leave(2 * j + 1, pl.ds(j * half, half), grad, grad_hbm)
    for copy in copies:
        copy.wait()


def sum_all(flat):
    part = lax.all_to_all(flat.reshape(32, 9, 1, 128), PLANE, 0, 0).sum(0)
    part = lax.all_to_all(jnp.broadcast_to(part[None], (16, 9, 1, 128)), "z", 0, 0).sum(0)
    whole = lax.all_to_all(jnp.broadcast_to(part[None], (32, 9, 1, 128)), PLANE, 0, 0)
    return whole.reshape(288, 128)


VMEM = pl.BlockSpec(memory_space=pltpu.VMEM)
HBM = pl.BlockSpec(memory_space=pltpu.HBM)
PARAMS = pltpu.CompilerParams(vmem_limit_bytes=32 * 1024 * 1024)


def per_device(
    points,
    counts,
    norm_gain,
    w_fx,
    w_slice,
    temper,
    query_projection,
    key_projection,
    value_projection,
    w_out,
    cotangent,
):
    rows, width = points.shape
    gain = norm_gain.reshape(1, width)
    n = HEADS * SLICES
    kept = (points, gain, w_slice, w_fx, w_out, cotangent)
    projections = (query_projection, key_projection, value_projection)

    def like(*shapes):
        return tuple(jax.ShapeDtypeStruct(shape, kind) for shape, kind in shapes)

    flat, w_t, w_bf, c_t, scales, w_hi, w_lo, *kept = pl.pallas_call(
        front_kernel,
        out_shape=like(
            ((288, 128), F32),
            ((n, rows), F32),
            ((n, rows), BF16),
            ((n, rows), BF16),
            ((HEADS, rows), F32),
            ((n, 384), BF16),
            ((n, 384), BF16),
            *((a.shape, a.dtype) for a in kept),
        ),
        in_specs=[VMEM] + [HBM] * 10,
        out_specs=(VMEM,) * 13,
        scratch_shapes=[
            *(pltpu.VMEM(a.shape, F32) for a in projections),
            pltpu.SMEM((HEADS,), F32),
            pltpu.VMEM((n, rows), F32),
            pltpu.SemaphoreType.DMA((10,)),
        ],
        compiler_params=PARAMS,
        name="front",
    )(
        counts,
        *(pltpu.with_memory_space_constraint(a, pltpu.HBM) for a in (temper, *kept, *projections)),
    )
    return pl.pallas_call(
        back_kernel,
        out_shape=like(((rows, width), BF16), ((rows, width), BF16)),
        in_specs=[VMEM] * 13,
        out_specs=(HBM,) * 2,
        scratch_shapes=[
            pltpu.VMEM((rows, width), BF16),
            pltpu.VMEM((rows, width), BF16),
            pltpu.VMEM((n, rows), BF16),
            pltpu.VMEM((width, rows), BF16),
            pltpu.VMEM((width, rows), F32),
            pltpu.SemaphoreType.DMA((4,)),
        ],
        compiler_params=PARAMS,
        name="back",
    )(sum_all(flat), w_t, w_bf, c_t, scales, *kept, w_hi, w_lo)


def solution(mesh):
    fine = Mesh(mesh.devices.reshape(16, 2, 2, 2, 4), ALL)
    rows = P(ALL, None)
    return jax.shard_map(
        per_device,
        mesh=fine,
        in_specs=(rows, P(("z", "xh", "c"), ("xl", "y"))) + (P(),) * 8 + (rows,),
        out_specs=(rows, rows),
        check_vma=False,
    )
```

```python
import math

import jax
import jax.numpy as jnp
from jax import lax
from jax.experimental import pallas as pl
from jax.experimental.pallas import tpu as pltpu
from jax.sharding import Mesh, PartitionSpec as P

PLANE = ("xh", "c", "xl", "y")
ALL = ("z", "xh", "c", "xl", "y")
HEADS, SLICES, DH = 8, 64, 32
Z_ORDER = [8, 9, 10, 11, 12, 13, 14, 15, 0, 1, 2, 3, 4, 5, 6, 7]
PLANE_ORDER = [18, 0, 1, 2, 3, 4, 5, 6, 7, 8, 9, 10, 11, 12, 13, 14, 15, 16, 17, 19, 20, 21, 22, 23, 24, 25, 26, 27, 28, 29, 30, 31]
F32, BF16 = jnp.float32, jnp.bfloat16


def dot(a, b, ca, cb, precision=None):
    return lax.dot_general(
        a, b, (((ca,), (cb,)), ((), ())), precision=precision, preferred_element_type=F32
    )


def parts(a):
    hi = a.astype(BF16)
    return hi, (a - hi.astype(F32)).astype(BF16)


def dot3(a, b, ca, cb):
    n = b[0].shape[1 - cb]
    left = jnp.concatenate(a, ca)
    right = jnp.concatenate([jnp.concatenate([b[0], b[0]], cb), jnp.concatenate([b[1], jnp.zeros_like(b[1])], cb)], 1 - cb)
    both = dot(left, right, ca, cb)
    return both[:, :n] + both[:, n:]


def normalise(x):
    cent = x - jnp.mean(x, -1, keepdims=True)
    rstd = lax.rsqrt(jnp.mean(cent * cent, -1, keepdims=True) + 1e-05)
    return cent * rstd, rstd


def front_kernel(*refs):
    count, temper_hbm = refs[:2]
    sources = refs[2:11]
    flat, whole, w_bf, c_t, scales, w_hi, w_lo = refs[11:18]
    temper, logit_t, sems = refs[27:30]
    targets = refs[18:24] + refs[24:27]
    x_ref, gain, w_slice, w_fx, w_out, cot = targets[:6]
    rows = x_ref.shape[0]
    copies = [
        pltpu.make_async_copy(a, b, sems.at[i])
        for i, (a, b) in enumerate(zip((*sources, temper_hbm), (*targets, temper)))
    ]
    for copy in copies:
        copy.start()
    copies[0].wait()
    copies[1].wait()
    normed = (normalise(x_ref[...].astype(F32))[0] * gain[...]).astype(BF16)
    for copy in copies[2:]:
        copy.wait()
    logit_t[...] = dot(w_slice[...].T, normed, 1, 1)
    stack_weights(*targets[6:], w_hi, w_lo)
    feats = dot(w_fx[...].T, normed, 1, 1).astype(BF16)
    gmix = dot(w_out[...], cot[...], 1, 1).astype(BF16)
    for h in range(HEADS):
        c_t[h * 64 : h * 64 + 32, :] = feats[h * 32 : h * 32 + 32, :]
        c_t[h * 64 + 32 : h * 64 + 64, :] = gmix[h * 32 : h * 32 + 32, :]
    live = (lax.broadcasted_iota(jnp.int32, (1, rows), 1) < count[...]).astype(F32)
    for h in range(HEADS):
        part = slice(h * SLICES, (h + 1) * SLICES)
        logits = logit_t[part, :]
        scale = 1.0 / jnp.full((1, rows), temper[h], F32)
        scales[h : h + 1, :] = scale
        e = jnp.exp((logits - jnp.max(logits, 0, keepdims=True)) * scale)
        w = e * (live / jnp.sum(e, 0, keepdims=True))
        w = w.astype(BF16)
        w_bf[part, :] = w
        whole[h : h + 1, :] = 1.0 / jnp.maximum(jnp.sum(w.astype(F32), 0, keepdims=True), 0.5)
    lane = lax.broadcasted_iota(jnp.int32, (64, 128), 1)
    for p in range(4):
        part = slice(p * 128, (p + 1) * 128)
        both = dot(w_bf[part, :], c_t[part, :], 1, 1)
        flat[p * 64 : (p + 1) * 64, :] = jnp.where(lane < 64, both[:64], both[64:])
    den = dot(jnp.ones((8, rows), BF16), w_bf[...], 1, 1)
    flat[256:288, :] = jnp.zeros((32, 128), F32)
    for p in range(4):
        flat[256 + p : 257 + p, :] = den[0:1, p * 128 : (p + 1) * 128]


def stack_weights(query, key, value, hi, lo):
    for h in range(HEADS):
        q, k, v = query[h], key[h], value[h]
        a, a_t, v_t = dot3(parts(q), parts(k), 1, 1), dot3(parts(k), parts(q), 1, 1), v.T
        none, gap = jnp.zeros((32, 32), F32), jnp.zeros((32, 64), F32)

        def at(left, right):
            block = jnp.concatenate([left, right], 1)
            return [block, gap] if h % 2 == 0 else [gap, block]

        upper = jnp.concatenate([*at(a, v), *at(a_t, none), gap, gap], 1)
        lower = jnp.concatenate([gap, gap, gap, gap, *at(v_t, none)], 1)
        whole = jnp.concatenate([upper, lower], 0)
        for ref, part in zip((hi, lo), parts(whole)):
            ref[h * 64 : (h + 1) * 64, :] = part


def middle(flat, w_hi, w_lo):
    row = lax.broadcasted_iota(jnp.int32, (128, 128), 0)
    lane = lax.broadcasted_iota(jnp.int32, (128, 128), 1)
    own = row // 64 == lane // 64
    second = (lane // 32) % 2 == 1
    scale = 1.0 / math.sqrt(DH)
    pairs = range(4)

    def each(f, *lists):
        return [f(*items) for items in zip(*lists)]

    def part(p):
        return slice(p * 128, (p + 1) * 128)

    t = [flat[p * 64 : (p + 1) * 64, :] for p in pairs]
    t = each(lambda t: jnp.where(own, jnp.concatenate([t, t], 0), 0.0), t)
    num = each(lambda t: jnp.where(second, 0.0, t), t)
    rec = 1.0 / (flat[256:264, :] + 1e-05)
    along = [rec[p : p + 1, :] for p in pairs]
    rec = rec.T
    down = [rec[:, p : p + 1] for p in pairs]
    split = each(parts, t)
    raw = [dot3(split[p], (w_hi[part(p), :], w_lo[part(p), :]), 1, 0) for p in pairs]
    u_v, u_t, g_v = (each(lambda a: parts(a[:, part(i)]), raw) for i in range(3))
    num_split = each(parts, num)
    s = each(
        lambda u, n, a, d: jnp.where(own, dot3(u, n, 1, 1) * (scale * a) * d, -jnp.inf),
        u_v, num_split, along, down,
    )
    g_prob = each(lambda g, n, a: dot3(g, n, 1, 1) * a, g_v, num_split, along)
    e = each(lambda s: jnp.exp(s - jnp.max(s, -1, keepdims=True)), s)
    prob = each(lambda e: e * (1.0 / jnp.sum(e, -1, keepdims=True)), e)
    g_s = each(lambda w, g: w * (g - jnp.sum(w * g, -1, keepdims=True)) * scale, prob, g_prob)
    g_tok = each(
        lambda g, w, u_v, u_t, g_v, a, d: dot3(parts(g * a), u_t, 1, 0)
        + dot3(parts(g * d), u_v, 0, 0)
        + dot3(parts(w), g_v, 0, 0),
        g_s, prob, u_v, u_t, g_v, along, down,
    )
    att = each(lambda w, a, v: dot3(parts(w * a), v, 1, 0), prob, along, u_v)
    blocks = each(lambda a, g, d: jnp.where(second, a, g * d), att, g_tok, down)
    g_den = each(lambda n, b, d: -jnp.sum(n * b, -1, keepdims=True) * d, num, blocks, down)
    return blocks, g_den


def back_kernel(
    flat, whole, w_bf, c_t, scales, x_ref, gain, w_slice, w_fx, w_out, cot, w_hi, w_lo,
    updated_hbm, grad_hbm, updated, grad, g_logit, g_feat, mixed_t, sems,
):
    blocks, g_den = middle(flat, w_hi, w_lo)
    split = [parts(b) for b in blocks]
    total, width = x_ref.shape
    half = total // 2
    copies = []

    def leave(i, at, source, target):
        copies.append(pltpu.make_async_copy(source.at[at], target.at[at], sems.at[i]))
        copies[-1].start()

    for j in range(2):
        at = slice(j * half, (j + 1) * half)
        for p in range(4):
            part = slice(p * 128, (p + 1) * 128)
            c = c_t[part, at]
            g_w = dot(jnp.concatenate(split[p], 1), jnp.concatenate([c, c], 0), 1, 0) + g_den[p]
            both = dot(split[p][0], w_bf[part, at], 0, 0)
            for i in range(2):
                h = 2 * p + i
                mine = slice(h * SLICES, (h + 1) * SLICES)
                w, g = w_bf[mine, at].astype(F32), g_w[i * 64 : (i + 1) * 64]
                mean = jnp.sum(w * g, 0, keepdims=True) * whole[h : h + 1, at]
                g_logit[mine, at] = (w * (g - mean) * scales[h : h + 1, at]).astype(BF16)
                g_feat[h * 32 : (h + 1) * 32, at] = both[i * 64 : i * 64 + 32].astype(BF16)
                mixed_t[h * 32 : (h + 1) * 32, at] = both[i * 64 + 32 : i * 64 + 64]
        x = x_ref[at, :].astype(F32)
        mixed = mixed_t[:, at].T.astype(BF16)
        updated[at, :] = (x + dot(mixed, w_out[...], 1, 0)).astype(BF16)
        leave(2 * j, pl.ds(j * half, half), updated, updated_hbm)
        g_normed = dot(w_slice[...], g_logit[:, at], 1, 0) + dot(w_fx[...], g_feat[:, at], 1, 0)
        g_normed = g_normed.T.astype(BF16).astype(F32)
        hat, rstd = normalise(x)
        g_hat = g_normed * gain[...]
        along = jnp.mean(g_hat * hat, -1, keepdims=True)
        g_x = rstd * (g_hat - jnp.mean(g_hat, -1, keepdims=True) - hat * along)
        grad[at, :] = (cot[at, :].astype(F32) + g_x).astype(BF16)
        leave(2 * j + 1, pl.ds(j * half, half), grad, grad_hbm)
    for copy in copies:
        copy.wait()


def sum_all(flat):
    def trade(parts, axis, order):
        return lax.all_to_all(parts, axis, 0, 0, axis_index_groups=[order])

    part = trade(flat.reshape(32, 9, 1, 128), PLANE, PLANE_ORDER).sum(0)
    part = trade(jnp.broadcast_to(part[None], (16, 9, 1, 128)), "z", Z_ORDER).sum(0)
    whole = trade(jnp.broadcast_to(part[None], (32, 9, 1, 128)), PLANE, PLANE_ORDER)
    return whole.reshape(288, 128)


VMEM = pl.BlockSpec(memory_space=pltpu.VMEM)
HBM = pl.BlockSpec(memory_space=pltpu.HBM)
PARAMS = pltpu.CompilerParams(vmem_limit_bytes=32 * 1024 * 1024)


def per_device(
    points,
    counts,
    norm_gain,
    w_fx,
    w_slice,
    temper,
    query_projection,
    key_projection,
    value_projection,
    w_out,
    cotangent,
):
    rows, width = points.shape
    gain = norm_gain.reshape(1, width)
    n = HEADS * SLICES
    kept = (points, gain, w_slice, w_fx, w_out, cotangent)
    projections = (query_projection, key_projection, value_projection)

    def like(*shapes):
        return tuple(jax.ShapeDtypeStruct(shape, kind) for shape, kind in shapes)

    flat, whole, w_bf, c_t, scales, w_hi, w_lo, *kept = pl.pallas_call(
        front_kernel,
        out_shape=like(
            ((288, 128), F32),
            ((HEADS, rows), F32),
            ((n, rows), BF16),
            ((n, rows), BF16),
            ((HEADS, rows), F32),
            ((n, 384), BF16),
            ((n, 384), BF16),
            *((a.shape, a.dtype) for a in kept),
        ),
        in_specs=[VMEM] + [HBM] * 10,
        out_specs=(VMEM,) * 13,
        scratch_shapes=[
            *(pltpu.VMEM(a.shape, F32) for a in projections),
            pltpu.SMEM((HEADS,), F32),
            pltpu.VMEM((n, rows), F32),
            pltpu.SemaphoreType.DMA((10,)),
        ],
        compiler_params=PARAMS,
        name="front",
    )(
        counts,
        *(pltpu.with_memory_space_constraint(a, pltpu.HBM) for a in (temper, *kept, *projections)),
    )
    return pl.pallas_call(
        back_kernel,
        out_shape=like(((rows, width), BF16), ((rows, width), BF16)),
        in_specs=[VMEM] * 13,
        out_specs=(HBM,) * 2,
        scratch_shapes=[
            pltpu.VMEM((rows, width), BF16),
            pltpu.VMEM((rows, width), BF16),
            pltpu.VMEM((n, rows), BF16),
            pltpu.VMEM((width, rows), BF16),
            pltpu.VMEM((width, rows), F32),
            pltpu.SemaphoreType.DMA((4,)),
        ],
        compiler_params=PARAMS,
        name="back",
    )(sum_all(flat), whole, w_bf, c_t, scales, *kept, w_hi, w_lo)


def solution(mesh):
    fine = Mesh(mesh.devices.reshape(16, 2, 2, 2, 4), ALL)
    rows = P(ALL, None)
    return jax.shard_map(
        per_device,
        mesh=fine,
        in_specs=(rows, P(("z", "xh", "c"), ("xl", "y"))) + (P(),) * 8 + (rows,),
        out_specs=(rows, rows),
        check_vma=False,
    )
```

```python
import math

import jax
import jax.numpy as jnp
from jax import lax
from jax.experimental import pallas as pl
from jax.experimental.pallas import tpu as pltpu
from jax.sharding import Mesh, PartitionSpec as P

PLANE = ("xh", "c", "xl", "y")
ALL = ("z", "xh", "c", "xl", "y")
HEADS, SLICES, DH = 8, 64, 32
Z_ORDER = [8, 9, 7, 10, 6, 11, 5, 12, 4, 13, 3, 14, 2, 15, 1, 0]
PLANE_ORDER = [26, *range(26), *range(27, 32)]
F32, BF16 = jnp.float32, jnp.bfloat16


def dot(a, b, ca, cb, precision=None):
    return lax.dot_general(
        a, b, (((ca,), (cb,)), ((), ())), precision=precision, preferred_element_type=F32
    )


def parts(a):
    hi = a.astype(BF16)
    return hi, (a - hi.astype(F32)).astype(BF16)


def dot3(a, b, ca, cb):
    n = b[0].shape[1 - cb]
    left = jnp.concatenate(a, ca)
    right = jnp.concatenate([jnp.concatenate([b[0], b[0]], cb), jnp.concatenate([b[1], jnp.zeros_like(b[1])], cb)], 1 - cb)
    both = dot(left, right, ca, cb)
    return both[:, :n] + both[:, n:]


def normalise(x):
    cent = x - jnp.mean(x, -1, keepdims=True)
    rstd = lax.rsqrt(jnp.mean(cent * cent, -1, keepdims=True) + 1e-05)
    return cent * rstd, rstd


def front_kernel(*refs):
    count, temper_hbm = refs[:2]
    sources = refs[2:11]
    flat, whole, w_bf, c_t, scales, w_hi, w_lo = refs[11:18]
    temper, logit_t, sems = refs[27:30]
    targets = refs[18:24] + refs[24:27]
    x_ref, gain, w_slice, w_fx, w_out, cot = targets[:6]
    rows = x_ref.shape[0]
    copies = [
        pltpu.make_async_copy(a, b, sems.at[i])
        for i, (a, b) in enumerate(zip((*sources, temper_hbm), (*targets, temper)))
    ]
    for copy in copies:
        copy.start()
    copies[0].wait()
    copies[1].wait()
    normed = (normalise(x_ref[...].astype(F32))[0] * gain[...]).astype(BF16)
    for copy in copies[2:]:
        copy.wait()
    logit_t[...] = dot(w_slice[...].T, normed, 1, 1)
    stack_weights(*targets[6:], w_hi, w_lo)
    feats = dot(w_fx[...].T, normed, 1, 1).astype(BF16)
    gmix = dot(w_out[...], cot[...], 1, 1).astype(BF16)
    for h in range(HEADS):
        c_t[h * 64 : h * 64 + 32, :] = feats[h * 32 : h * 32 + 32, :]
        c_t[h * 64 + 32 : h * 64 + 64, :] = gmix[h * 32 : h * 32 + 32, :]
    live = (lax.broadcasted_iota(jnp.int32, (1, rows), 1) < count[...]).astype(F32)
    for h in range(HEADS):
        part = slice(h * SLICES, (h + 1) * SLICES)
        logits = logit_t[part, :]
        scale = 1.0 / jnp.full((1, rows), temper[h], F32)
        scales[h : h + 1, :] = scale
        e = jnp.exp((logits - jnp.max(logits, 0, keepdims=True)) * scale)
        w = e * (live / jnp.sum(e, 0, keepdims=True))
        w = w.astype(BF16)
        w_bf[part, :] = w
        whole[h : h + 1, :] = 1.0 / jnp.maximum(jnp.sum(w.astype(F32), 0, keepdims=True), 0.5)
    lane = lax.broadcasted_iota(jnp.int32, (64, 128), 1)
    for p in range(4):
        part = slice(p * 128, (p + 1) * 128)
        both = dot(w_bf[part, :], c_t[part, :], 1, 1)
        flat[p * 64 : (p + 1) * 64, :] = jnp.where(lane < 64, both[:64], both[64:])
    den = dot(jnp.ones((8, rows), BF16), w_bf[...], 1, 1)
    flat[256:288, :] = jnp.zeros((32, 128), F32)
    for p in range(4):
        flat[256 + p : 257 + p, :] = den[0:1, p * 128 : (p + 1) * 128]


def stack_weights(query, key, value, hi, lo):
    for h in range(HEADS):
        q, k, v = query[h], key[h], value[h]
        a, a_t, v_t = dot3(parts(q), parts(k), 1, 1), dot3(parts(k), parts(q), 1, 1), v.T
        none, gap = jnp.zeros((32, 32), F32), jnp.zeros((32, 64), F32)

        def at(left, right):
            block = jnp.concatenate([left, right], 1)
            return [block, gap] if h % 2 == 0 else [gap, block]

        upper = jnp.concatenate([*at(a, v), *at(a_t, none), gap, gap], 1)
        lower = jnp.concatenate([gap, gap, gap, gap, *at(v_t, none)], 1)
        whole = jnp.concatenate([upper, lower], 0)
        for ref, part in zip((hi, lo), parts(whole)):
            ref[h * 64 : (h + 1) * 64, :] = part


def middle(flat, w_hi, w_lo):
    row = lax.broadcasted_iota(jnp.int32, (128, 128), 0)
    lane = lax.broadcasted_iota(jnp.int32, (128, 128), 1)
    own = row // 64 == lane // 64
    second = (lane // 32) % 2 == 1
    scale = 1.0 / math.sqrt(DH)
    pairs = range(4)

    def each(f, *lists):
        return [f(*items) for items in zip(*lists)]

    def part(p):
        return slice(p * 128, (p + 1) * 128)

    t = [flat[p * 64 : (p + 1) * 64, :] for p in pairs]
    t = each(lambda t: jnp.where(own, jnp.concatenate([t, t], 0), 0.0), t)
    num = each(lambda t: jnp.where(second, 0.0, t), t)
    rec = 1.0 / (flat[256:264, :] + 1e-05)
    along = [rec[p : p + 1, :] for p in pairs]
    rec = rec.T
    down = [rec[:, p : p + 1] for p in pairs]
    split = each(parts, t)
    raw = [dot3(split[p], (w_hi[part(p), :], w_lo[part(p), :]), 1, 0) for p in pairs]
    u_v, u_t, g_v = (each(lambda a: parts(a[:, part(i)]), raw) for i in range(3))
    num_split = each(parts, num)
    s = each(
        lambda u, n, a, d: jnp.where(own, dot3(u, n, 1, 1) * (scale * a) * d, -jnp.inf),
        u_v, num_split, along, down,
    )
    g_prob = each(lambda g, n, a: dot3(g, n, 1, 1) * a, g_v, num_split, along)
    e = each(lambda s: jnp.exp(s - jnp.max(s, -1, keepdims=True)), s)
    prob = each(lambda e: e * (1.0 / jnp.sum(e, -1, keepdims=True)), e)
    g_s = each(lambda w, g: w * (g - jnp.sum(w * g, -1, keepdims=True)) * scale, prob, g_prob)
    g_tok = each(
        lambda g, w, u_v, u_t, g_v, a, d: dot3(parts(g * a), u_t, 1, 0)
        + dot3(parts(g * d), u_v, 0, 0)
        + dot3(parts(w), g_v, 0, 0),
        g_s, prob, u_v, u_t, g_v, along, down,
    )
    att = each(lambda w, a, v: dot3(parts(w * a), v, 1, 0), prob, along, u_v)
    blocks = each(lambda a, g, d: jnp.where(second, a, g * d), att, g_tok, down)
    g_den = each(lambda n, b, d: -jnp.sum(n * b, -1, keepdims=True) * d, num, blocks, down)
    return blocks, g_den


def back_kernel(
    flat, whole, w_bf, c_t, scales, x_ref, gain, w_slice, w_fx, w_out, cot, w_hi, w_lo,
    updated_hbm, grad_hbm, updated, grad, g_logit, g_feat, mixed_t, sems,
):
    blocks, g_den = middle(flat, w_hi, w_lo)
    split = [parts(b) for b in blocks]
    total, width = x_ref.shape
    half = total // 2
    copies = []

    def leave(i, at, source, target):
        copies.append(pltpu.make_async_copy(source.at[at], target.at[at], sems.at[i]))
        copies[-1].start()

    for j in range(2):
        at = slice(j * half, (j + 1) * half)
        for p in range(4):
            part = slice(p * 128, (p + 1) * 128)
            c = c_t[part, at]
            g_w = dot(jnp.concatenate(split[p], 1), jnp.concatenate([c, c], 0), 1, 0) + g_den[p]
            both = dot(split[p][0], w_bf[part, at], 0, 0)
            for i in range(2):
                h = 2 * p + i
                mine = slice(h * SLICES, (h + 1) * SLICES)
                w, g = w_bf[mine, at].astype(F32), g_w[i * 64 : (i + 1) * 64]
                mean = jnp.sum(w * g, 0, keepdims=True) * whole[h : h + 1, at]
                g_logit[mine, at] = (w * (g - mean) * scales[h : h + 1, at]).astype(BF16)
                g_feat[h * 32 : (h + 1) * 32, at] = both[i * 64 : i * 64 + 32].astype(BF16)
                mixed_t[h * 32 : (h + 1) * 32, at] = both[i * 64 + 32 : i * 64 + 64]
        x = x_ref[at, :].astype(F32)
        mixed = mixed_t[:, at].T.astype(BF16)
        updated[at, :] = (x + dot(mixed, w_out[...], 1, 0)).astype(BF16)
        leave(2 * j, pl.ds(j * half, half), updated, updated_hbm)
        g_normed = dot(w_slice[...], g_logit[:, at], 1, 0) + dot(w_fx[...], g_feat[:, at], 1, 0)
        g_normed = g_normed.T.astype(BF16).astype(F32)
        hat, rstd = normalise(x)
        g_hat = g_normed * gain[...]
        along = jnp.mean(g_hat * hat, -1, keepdims=True)
        g_x = rstd * (g_hat - jnp.mean(g_hat, -1, keepdims=True) - hat * along)
        grad[at, :] = (cot[at, :].astype(F32) + g_x).astype(BF16)
        leave(2 * j + 1, pl.ds(j * half, half), grad, grad_hbm)
    for copy in copies:
        copy.wait()


def sum_all(flat):
    def trade(parts, axis, order):
        return lax.all_to_all(parts, axis, 0, 0, axis_index_groups=[order])

    part = trade(flat.reshape(32, 9, 1, 128), PLANE, PLANE_ORDER).sum(0)
    part = trade(jnp.broadcast_to(part[None], (16, 9, 1, 128)), "z", Z_ORDER).sum(0)
    whole = trade(jnp.broadcast_to(part[None], (32, 9, 1, 128)), PLANE, PLANE_ORDER)
    return whole.reshape(288, 128)


VMEM = pl.BlockSpec(memory_space=pltpu.VMEM)
HBM = pl.BlockSpec(memory_space=pltpu.HBM)
PARAMS = pltpu.CompilerParams(vmem_limit_bytes=32 * 1024 * 1024)


def per_device(
    points,
    counts,
    norm_gain,
    w_fx,
    w_slice,
    temper,
    query_projection,
    key_projection,
    value_projection,
    w_out,
    cotangent,
):
    rows, width = points.shape
    gain = norm_gain.reshape(1, width)
    n = HEADS * SLICES
    kept = (points, gain, w_slice, w_fx, w_out, cotangent)
    projections = (query_projection, key_projection, value_projection)

    def like(*shapes):
        return tuple(jax.ShapeDtypeStruct(shape, kind) for shape, kind in shapes)

    flat, whole, w_bf, c_t, scales, w_hi, w_lo, *kept = pl.pallas_call(
        front_kernel,
        out_shape=like(
            ((288, 128), F32),
            ((HEADS, rows), F32),
            ((n, rows), BF16),
            ((n, rows), BF16),
            ((HEADS, rows), F32),
            ((n, 384), BF16),
            ((n, 384), BF16),
            *((a.shape, a.dtype) for a in kept),
        ),
        in_specs=[VMEM] + [HBM] * 10,
        out_specs=(VMEM,) * 13,
        scratch_shapes=[
            *(pltpu.VMEM(a.shape, F32) for a in projections),
            pltpu.SMEM((HEADS,), F32),
            pltpu.VMEM((n, rows), F32),
            pltpu.SemaphoreType.DMA((10,)),
        ],
        compiler_params=PARAMS,
        name="front",
    )(
        counts,
        *(pltpu.with_memory_space_constraint(a, pltpu.HBM) for a in (temper, *kept, *projections)),
    )
    return pl.pallas_call(
        back_kernel,
        out_shape=like(((rows, width), BF16), ((rows, width), BF16)),
        in_specs=[VMEM] * 13,
        out_specs=(HBM,) * 2,
        scratch_shapes=[
            pltpu.VMEM((rows, width), BF16),
            pltpu.VMEM((rows, width), BF16),
            pltpu.VMEM((n, rows), BF16),
            pltpu.VMEM((width, rows), BF16),
            pltpu.VMEM((width, rows), F32),
            pltpu.SemaphoreType.DMA((4,)),
        ],
        compiler_params=PARAMS,
        name="back",
    )(sum_all(flat), whole, w_bf, c_t, scales, *kept, w_hi, w_lo)


def solution(mesh):
    fine = Mesh(mesh.devices.reshape(16, 2, 2, 2, 4), ALL)
    rows = P(ALL, None)
    return jax.shard_map(
        per_device,
        mesh=fine,
        in_specs=(rows, P(("z", "xh", "c"), ("xl", "y"))) + (P(),) * 8 + (rows,),
        out_specs=(rows, rows),
        check_vma=False,
    )
```

```python
import math

import jax
import jax.numpy as jnp
from jax import lax
from jax.experimental import pallas as pl
from jax.experimental.pallas import tpu as pltpu
from jax.sharding import Mesh, PartitionSpec as P

PLANE = ("xh", "c", "xl", "y")
ALL = ("z", "xh", "c", "xl", "y")
HEADS, SLICES, DH = 8, 64, 32
Z_ORDER = [8, 9, 7, 10, 6, 11, 5, 12, 4, 13, 3, 14, 2, 15, 1, 0]
PLANE_ORDER = [26, *range(26), *range(27, 32)]
F32, BF16 = jnp.float32, jnp.bfloat16


def dot(a, b, ca, cb, precision=None):
    return lax.dot_general(
        a, b, (((ca,), (cb,)), ((), ())), precision=precision, preferred_element_type=F32
    )


def parts(a):
    hi = a.astype(BF16)
    return hi, (a - hi.astype(F32)).astype(BF16)


def dot3(a, b, ca, cb):
    n = b[0].shape[1 - cb]
    left = jnp.concatenate(a, ca)
    right = jnp.concatenate([jnp.concatenate([b[0], b[0]], cb), jnp.concatenate([b[1], jnp.zeros_like(b[1])], cb)], 1 - cb)
    both = dot(left, right, ca, cb)
    return both[:, :n] + both[:, n:]


def normalise(x):
    cent = x - jnp.mean(x, -1, keepdims=True)
    rstd = lax.rsqrt(jnp.mean(cent * cent, -1, keepdims=True) + 1e-05)
    return cent * rstd, rstd


def front_kernel(*refs):
    count, temper_hbm = refs[:2]
    sources = refs[2:11]
    flat, whole, w_bf, c_t, scales, w_hi, w_lo = refs[11:18]
    temper, logit_t, sems = refs[27:30]
    targets = refs[18:24] + refs[24:27]
    x_ref, gain, w_slice, w_fx, w_out, cot = targets[:6]
    rows = x_ref.shape[0]
    copies = [
        pltpu.make_async_copy(a, b, sems.at[i])
        for i, (a, b) in enumerate(zip((*sources, temper_hbm), (*targets, temper)))
    ]
    for copy in copies:
        copy.start()
    copies[0].wait()
    copies[1].wait()
    normed = (normalise(x_ref[...].astype(F32))[0] * gain[...]).astype(BF16)
    for copy in copies[2:]:
        copy.wait()
    logit_t[...] = dot(w_slice[...].T, normed, 1, 1)
    stack_weights(*targets[6:], w_hi, w_lo)
    feats = dot(w_fx[...].T, normed, 1, 1).astype(BF16)
    gmix = dot(w_out[...], cot[...], 1, 1).astype(BF16)
    for h in range(HEADS):
        c_t[h * 64 : h * 64 + 32, :] = feats[h * 32 : h * 32 + 32, :]
        c_t[h * 64 + 32 : h * 64 + 64, :] = gmix[h * 32 : h * 32 + 32, :]
    live = (lax.broadcasted_iota(jnp.int32, (1, rows), 1) < count[...]).astype(F32)
    for h in range(HEADS):
        part = slice(h * SLICES, (h + 1) * SLICES)
        logits = logit_t[part, :]
        scale = 1.0 / jnp.full((1, rows), temper[h], F32)
        scales[h : h + 1, :] = scale
        e = jnp.exp((logits - jnp.max(logits, 0, keepdims=True)) * scale)
        w = e * (live / jnp.sum(e, 0, keepdims=True))
        w = w.astype(BF16)
        w_bf[part, :] = w
        whole[h : h + 1, :] = 1.0 / jnp.maximum(jnp.sum(w.astype(F32), 0, keepdims=True), 0.5)
    lane = lax.broadcasted_iota(jnp.int32, (64, 128), 1)
    for p in range(4):
        part = slice(p * 128, (p + 1) * 128)
        both = dot(w_bf[part, :], c_t[part, :], 1, 1)
        flat[p * 64 : (p + 1) * 64, :] = jnp.where(lane < 64, both[:64], both[64:])
    den = jnp.sum(w_bf[...].astype(F32), 1, keepdims=True)
    den = jnp.broadcast_to(den, (den.shape[0], 128)).T
    flat[256:288, :] = jnp.zeros((32, 128), F32)
    for p in range(4):
        flat[256 + p : 257 + p, :] = den[0:1, p * 128 : (p + 1) * 128]


def stack_weights(query, key, value, hi, lo):
    for h in range(HEADS):
        q, k, v = query[h], key[h], value[h]
        a, a_t, v_t = dot3(parts(q), parts(k), 1, 1), dot3(parts(k), parts(q), 1, 1), v.T
        none, gap = jnp.zeros((32, 32), F32), jnp.zeros((32, 64), F32)

        def at(left, right):
            block = jnp.concatenate([left, right], 1)
            return [block, gap] if h % 2 == 0 else [gap, block]

        upper = jnp.concatenate([*at(a, v), *at(a_t, none), gap, gap], 1)
        lower = jnp.concatenate([gap, gap, gap, gap, *at(v_t, none)], 1)
        whole = jnp.concatenate([upper, lower], 0)
        for ref, part in zip((hi, lo), parts(whole)):
            ref[h * 64 : (h + 1) * 64, :] = part


def middle(flat, w_hi, w_lo):
    row = lax.broadcasted_iota(jnp.int32, (128, 128), 0)
    lane = lax.broadcasted_iota(jnp.int32, (128, 128), 1)
    own = row // 64 == lane // 64
    second = (lane // 32) % 2 == 1
    scale = 1.0 / math.sqrt(DH)
    pairs = range(4)

    def each(f, *lists):
        return [f(*items) for items in zip(*lists)]

    def part(p):
        return slice(p * 128, (p + 1) * 128)

    t = [flat[p * 64 : (p + 1) * 64, :] for p in pairs]
    t = each(lambda t: jnp.where(own, jnp.concatenate([t, t], 0), 0.0), t)
    num = each(lambda t: jnp.where(second, 0.0, t), t)
    rec = 1.0 / (flat[256:264, :] + 1e-05)
    along = [rec[p : p + 1, :] for p in pairs]
    rec = rec.T
    down = [rec[:, p : p + 1] for p in pairs]
    split = each(parts, t)
    raw = [dot3(split[p], (w_hi[part(p), :], w_lo[part(p), :]), 1, 0) for p in pairs]
    u_v, u_t, g_v = (each(lambda a: parts(a[:, part(i)]), raw) for i in range(3))
    num_split = each(parts, num)
    s = each(
        lambda u, n, a, d: jnp.where(own, dot3(u, n, 1, 1) * (scale * a) * d, -jnp.inf),
        u_v, num_split, along, down,
    )
    g_prob = each(lambda g, n, a: dot3(g, n, 1, 1) * a, g_v, num_split, along)
    e = each(lambda s: jnp.exp(s - jnp.max(s, -1, keepdims=True)), s)
    prob = each(lambda e: e * (1.0 / jnp.sum(e, -1, keepdims=True)), e)
    g_s = each(lambda w, g: w * (g - jnp.sum(w * g, -1, keepdims=True)) * scale, prob, g_prob)
    g_tok = each(
        lambda g, w, u_v, u_t, g_v, a, d: dot3(parts(g * a), u_t, 1, 0)
        + dot3(parts(g * d), u_v, 0, 0)
        + dot3(parts(w), g_v, 0, 0),
        g_s, prob, u_v, u_t, g_v, along, down,
    )
    att = each(lambda w, a, v: dot3(parts(w * a), v, 1, 0), prob, along, u_v)
    blocks = each(lambda a, g, d: jnp.where(second, a, g * d), att, g_tok, down)
    g_den = each(lambda n, b, d: -jnp.sum(n * b, -1, keepdims=True) * d, num, blocks, down)
    return blocks, g_den


def back_kernel(
    flat, whole, w_bf, c_t, scales, x_ref, gain, w_slice, w_fx, w_out, cot, w_hi, w_lo,
    updated_hbm, grad_hbm, updated, grad, g_logit, g_feat, mixed_t, sems,
):
    blocks, g_den = middle(flat, w_hi, w_lo)
    split = [parts(b) for b in blocks]
    total, width = x_ref.shape
    half = total // 2
    copies = []

    def leave(i, at, source, target):
        copies.append(pltpu.make_async_copy(source.at[at], target.at[at], sems.at[i]))
        copies[-1].start()

    for j in range(2):
        at = slice(j * half, (j + 1) * half)
        for p in range(4):
            part = slice(p * 128, (p + 1) * 128)
            c = c_t[part, at]
            g_w = dot(jnp.concatenate(split[p], 1), jnp.concatenate([c, c], 0), 1, 0) + g_den[p]
            both = dot(split[p][0], w_bf[part, at], 0, 0)
            for i in range(2):
                h = 2 * p + i
                mine = slice(h * SLICES, (h + 1) * SLICES)
                w, g = w_bf[mine, at].astype(F32), g_w[i * 64 : (i + 1) * 64]
                mean = jnp.sum(w * g, 0, keepdims=True) * whole[h : h + 1, at]
                g_logit[mine, at] = (w * (g - mean) * scales[h : h + 1, at]).astype(BF16)
                g_feat[h * 32 : (h + 1) * 32, at] = both[i * 64 : i * 64 + 32].astype(BF16)
                mixed_t[h * 32 : (h + 1) * 32, at] = both[i * 64 + 32 : i * 64 + 64]
        x = x_ref[at, :].astype(F32)
        mixed = mixed_t[:, at].T.astype(BF16)
        updated[at, :] = (x + dot(mixed, w_out[...], 1, 0)).astype(BF16)
        leave(2 * j, pl.ds(j * half, half), updated, updated_hbm)
        g_normed = dot(w_slice[...], g_logit[:, at], 1, 0) + dot(w_fx[...], g_feat[:, at], 1, 0)
        g_normed = g_normed.T.astype(BF16).astype(F32)
        hat, rstd = normalise(x)
        g_hat = g_normed * gain[...]
        along = jnp.mean(g_hat * hat, -1, keepdims=True)
        g_x = rstd * (g_hat - jnp.mean(g_hat, -1, keepdims=True) - hat * along)
        grad[at, :] = (cot[at, :].astype(F32) + g_x).astype(BF16)
        leave(2 * j + 1, pl.ds(j * half, half), grad, grad_hbm)
    for copy in copies:
        copy.wait()


def sum_all(flat):
    def trade(parts, axis, order):
        return lax.all_to_all(parts, axis, 0, 0, axis_index_groups=[order])

    part = trade(flat.reshape(32, 9, 1, 128), PLANE, PLANE_ORDER).sum(0)
    part = trade(jnp.broadcast_to(part[None], (16, 9, 1, 128)), "z", Z_ORDER).sum(0)
    whole = trade(jnp.broadcast_to(part[None], (32, 9, 1, 128)), PLANE, PLANE_ORDER)
    return whole.reshape(288, 128)


VMEM = pl.BlockSpec(memory_space=pltpu.VMEM)
HBM = pl.BlockSpec(memory_space=pltpu.HBM)
PARAMS = pltpu.CompilerParams(vmem_limit_bytes=32 * 1024 * 1024)


def per_device(
    points,
    counts,
    norm_gain,
    w_fx,
    w_slice,
    temper,
    query_projection,
    key_projection,
    value_projection,
    w_out,
    cotangent,
):
    rows, width = points.shape
    gain = norm_gain.reshape(1, width)
    n = HEADS * SLICES
    kept = (points, gain, w_slice, w_fx, w_out, cotangent)
    projections = (query_projection, key_projection, value_projection)

    def like(*shapes):
        return tuple(jax.ShapeDtypeStruct(shape, kind) for shape, kind in shapes)

    flat, whole, w_bf, c_t, scales, w_hi, w_lo, *kept = pl.pallas_call(
        front_kernel,
        out_shape=like(
            ((288, 128), F32),
            ((HEADS, rows), F32),
            ((n, rows), BF16),
            ((n, rows), BF16),
            ((HEADS, rows), F32),
            ((n, 384), BF16),
            ((n, 384), BF16),
            *((a.shape, a.dtype) for a in kept),
        ),
        in_specs=[VMEM] + [HBM] * 10,
        out_specs=(VMEM,) * 13,
        scratch_shapes=[
            *(pltpu.VMEM(a.shape, F32) for a in projections),
            pltpu.SMEM((HEADS,), F32),
            pltpu.VMEM((n, rows), F32),
            pltpu.SemaphoreType.DMA((10,)),
        ],
        compiler_params=PARAMS,
        name="front",
    )(
        counts,
        *(pltpu.with_memory_space_constraint(a, pltpu.HBM) for a in (temper, *kept, *projections)),
    )
    return pl.pallas_call(
        back_kernel,
        out_shape=like(((rows, width), BF16), ((rows, width), BF16)),
        in_specs=[VMEM] * 13,
        out_specs=(HBM,) * 2,
        scratch_shapes=[
            pltpu.VMEM((rows, width), BF16),
            pltpu.VMEM((rows, width), BF16),
            pltpu.VMEM((n, rows), BF16),
            pltpu.VMEM((width, rows), BF16),
            pltpu.VMEM((width, rows), F32),
            pltpu.SemaphoreType.DMA((4,)),
        ],
        compiler_params=PARAMS,
        name="back",
    )(sum_all(flat), whole, w_bf, c_t, scales, *kept, w_hi, w_lo)


def solution(mesh):
    fine = Mesh(mesh.devices.reshape(16, 2, 2, 2, 4), ALL)
    rows = P(ALL, None)
    return jax.shard_map(
        per_device,
        mesh=fine,
        in_specs=(rows, P(("z", "xh", "c"), ("xl", "y"))) + (P(),) * 8 + (rows,),
        out_specs=(rows, rows),
        check_vma=False,
    )
```

```python
import math

import jax
import jax.numpy as jnp
from jax import lax
from jax.experimental import pallas as pl
from jax.experimental.pallas import tpu as pltpu
from jax.sharding import Mesh, PartitionSpec as P

PLANE = ("xh", "c", "xl", "y")
ALL = ("z", "xh", "c", "xl", "y")
HEADS, SLICES, DH = 8, 64, 32
Z_ORDER = [8, 9, 7, 10, 6, 11, 5, 12, 4, 13, 3, 14, 2, 15, 1, 0]
PLANE_ORDER = [26, 18, *(i for i in range(32) if i not in (26, 18, 8)), 8]
F32, BF16 = jnp.float32, jnp.bfloat16


def dot(a, b, ca, cb, precision=None):
    return lax.dot_general(
        a, b, (((ca,), (cb,)), ((), ())), precision=precision, preferred_element_type=F32
    )


def parts(a):
    hi = a.astype(BF16)
    return hi, (a - hi.astype(F32)).astype(BF16)


def dot3(a, b, ca, cb):
    n = b[0].shape[1 - cb]
    left = jnp.concatenate(a, ca)
    right = jnp.concatenate([jnp.concatenate([b[0], b[0]], cb), jnp.concatenate([b[1], jnp.zeros_like(b[1])], cb)], 1 - cb)
    both = dot(left, right, ca, cb)
    return both[:, :n] + both[:, n:]


def normalise(x):
    cent = x - jnp.mean(x, -1, keepdims=True)
    rstd = lax.rsqrt(jnp.mean(cent * cent, -1, keepdims=True) + 1e-05)
    return cent * rstd, rstd


def front_kernel(*refs):
    count, temper_hbm = refs[:2]
    sources = refs[2:11]
    flat, whole, w_bf, c_t, scales, w_hi, w_lo = refs[11:18]
    temper, logit_t, sems = refs[27:30]
    targets = refs[18:24] + refs[24:27]
    x_ref, gain, w_slice, w_fx, w_out, cot = targets[:6]
    rows = x_ref.shape[0]
    copies = [
        pltpu.make_async_copy(a, b, sems.at[i])
        for i, (a, b) in enumerate(zip((*sources, temper_hbm), (*targets, temper)))
    ]
    for copy in copies:
        copy.start()
    copies[0].wait()
    copies[1].wait()
    normed = (normalise(x_ref[...].astype(F32))[0] * gain[...]).astype(BF16)
    for copy in copies[2:]:
        copy.wait()
    logit_t[...] = dot(w_slice[...].T, normed, 1, 1)
    stack_weights(*targets[6:], w_hi, w_lo)
    feats = dot(w_fx[...].T, normed, 1, 1).astype(BF16)
    gmix = dot(w_out[...], cot[...], 1, 1).astype(BF16)
    for h in range(HEADS):
        c_t[h * 64 : h * 64 + 32, :] = feats[h * 32 : h * 32 + 32, :]
        c_t[h * 64 + 32 : h * 64 + 64, :] = gmix[h * 32 : h * 32 + 32, :]
    live = (lax.broadcasted_iota(jnp.int32, (1, rows), 1) < count[...]).astype(F32)
    for h in range(HEADS):
        part = slice(h * SLICES, (h + 1) * SLICES)
        logits = logit_t[part, :]
        scale = 1.0 / jnp.full((1, rows), temper[h], F32)
        scales[h : h + 1, :] = scale
        e = jnp.exp((logits - jnp.max(logits, 0, keepdims=True)) * scale)
        w = e * (live / jnp.sum(e, 0, keepdims=True))
        w = w.astype(BF16)
        w_bf[part, :] = w
        whole[h : h + 1, :] = 1.0 / jnp.maximum(jnp.sum(w.astype(F32), 0, keepdims=True), 0.5)
    lane = lax.broadcasted_iota(jnp.int32, (64, 128), 1)
    for p in range(4):
        part = slice(p * 128, (p + 1) * 128)
        both = dot(w_bf[part, :], c_t[part, :], 1, 1)
        flat[p * 64 : (p + 1) * 64, :] = jnp.where(lane < 64, both[:64], both[64:])
    den = jnp.sum(w_bf[...].astype(F32), 1, keepdims=True)
    den = jnp.broadcast_to(den, (den.shape[0], 128)).T
    flat[256:288, :] = jnp.zeros((32, 128), F32)
    for p in range(4):
        flat[256 + p : 257 + p, :] = den[0:1, p * 128 : (p + 1) * 128]


def stack_weights(query, key, value, hi, lo):
    for h in range(HEADS):
        q, k, v = query[h], key[h], value[h]
        a, a_t, v_t = dot3(parts(q), parts(k), 1, 1), dot3(parts(k), parts(q), 1, 1), v.T
        none, gap = jnp.zeros((32, 32), F32), jnp.zeros((32, 64), F32)

        def at(left, right):
            block = jnp.concatenate([left, right], 1)
            return [block, gap] if h % 2 == 0 else [gap, block]

        upper = jnp.concatenate([*at(a, v), *at(a_t, none), gap, gap], 1)
        lower = jnp.concatenate([gap, gap, gap, gap, *at(v_t, none)], 1)
        whole = jnp.concatenate([upper, lower], 0)
        for ref, part in zip((hi, lo), parts(whole)):
            ref[h * 64 : (h + 1) * 64, :] = part


def middle(flat, w_hi, w_lo):
    row = lax.broadcasted_iota(jnp.int32, (128, 128), 0)
    lane = lax.broadcasted_iota(jnp.int32, (128, 128), 1)
    own = row // 64 == lane // 64
    second = (lane // 32) % 2 == 1
    scale = 1.0 / math.sqrt(DH)
    pairs = range(4)

    def each(f, *lists):
        return [f(*items) for items in zip(*lists)]

    def part(p):
        return slice(p * 128, (p + 1) * 128)

    t = [flat[p * 64 : (p + 1) * 64, :] for p in pairs]
    t = each(lambda t: jnp.where(own, jnp.concatenate([t, t], 0), 0.0), t)
    num = each(lambda t: jnp.where(second, 0.0, t), t)
    rec = 1.0 / (flat[256:264, :] + 1e-05)
    along = [rec[p : p + 1, :] for p in pairs]
    rec = rec.T
    down = [rec[:, p : p + 1] for p in pairs]
    split = each(parts, t)
    raw = [dot3(split[p], (w_hi[part(p), :], w_lo[part(p), :]), 1, 0) for p in pairs]
    u_v, u_t, g_v = (each(lambda a: parts(a[:, part(i)]), raw) for i in range(3))
    num_split = each(parts, num)
    s = each(
        lambda u, n, a, d: jnp.where(own, dot3(u, n, 1, 1) * (scale * a) * d, -jnp.inf),
        u_v, num_split, along, down,
    )
    g_prob = each(lambda g, n, a: dot3(g, n, 1, 1) * a, g_v, num_split, along)
    e = each(lambda s: jnp.exp(s - jnp.max(s, -1, keepdims=True)), s)
    prob = each(lambda e: e * (1.0 / jnp.sum(e, -1, keepdims=True)), e)
    g_s = each(lambda w, g: w * (g - jnp.sum(w * g, -1, keepdims=True)) * scale, prob, g_prob)
    g_tok = each(
        lambda g, w, u_v, u_t, g_v, a, d: dot3(parts(g * a), u_t, 1, 0)
        + dot3(parts(g * d), u_v, 0, 0)
        + dot3(parts(w), g_v, 0, 0),
        g_s, prob, u_v, u_t, g_v, along, down,
    )
    att = each(lambda w, a, v: dot3(parts(w * a), v, 1, 0), prob, along, u_v)
    blocks = each(lambda a, g, d: jnp.where(second, a, g * d), att, g_tok, down)
    g_den = each(lambda n, b, d: -jnp.sum(n * b, -1, keepdims=True) * d, num, blocks, down)
    return blocks, g_den


def back_kernel(
    flat, whole, w_bf, c_t, scales, x_ref, gain, w_slice, w_fx, w_out, cot, w_hi, w_lo,
    updated_hbm, grad_hbm, updated, grad, g_logit, g_feat, mixed_t, sems,
):
    hats = [normalise(x_ref[j * 256 : (j + 1) * 256, :].astype(F32)) for j in range(2)]
    blocks, g_den = middle(flat, w_hi, w_lo)
    split = [parts(b) for b in blocks]
    total, width = x_ref.shape
    half = total // 2
    copies = []

    def leave(i, at, source, target):
        copies.append(pltpu.make_async_copy(source.at[at], target.at[at], sems.at[i]))
        copies[-1].start()

    for j in range(2):
        at = slice(j * half, (j + 1) * half)
        for p in range(4):
            part = slice(p * 128, (p + 1) * 128)
            c = c_t[part, at]
            g_w = dot(jnp.concatenate(split[p], 1), jnp.concatenate([c, c], 0), 1, 0) + g_den[p]
            both = dot(split[p][0], w_bf[part, at], 0, 0)
            for i in range(2):
                h = 2 * p + i
                mine = slice(h * SLICES, (h + 1) * SLICES)
                w, g = w_bf[mine, at].astype(F32), g_w[i * 64 : (i + 1) * 64]
                mean = jnp.sum(w * g, 0, keepdims=True) * whole[h : h + 1, at]
                g_logit[mine, at] = (w * (g - mean) * scales[h : h + 1, at]).astype(BF16)
                g_feat[h * 32 : (h + 1) * 32, at] = both[i * 64 : i * 64 + 32].astype(BF16)
                mixed_t[h * 32 : (h + 1) * 32, at] = both[i * 64 + 32 : i * 64 + 64]
        x = x_ref[at, :].astype(F32)
        mixed = mixed_t[:, at].T.astype(BF16)
        updated[at, :] = (x + dot(mixed, w_out[...], 1, 0)).astype(BF16)
        leave(2 * j, pl.ds(j * half, half), updated, updated_hbm)
        g_normed = dot(w_slice[...], g_logit[:, at], 1, 0) + dot(w_fx[...], g_feat[:, at], 1, 0)
        g_normed = g_normed.T.astype(BF16).astype(F32)
        hat, rstd = hats[j]
        g_hat = g_normed * gain[...]
        along = jnp.mean(g_hat * hat, -1, keepdims=True)
        g_x = rstd * (g_hat - jnp.mean(g_hat, -1, keepdims=True) - hat * along)
        grad[at, :] = (cot[at, :].astype(F32) + g_x).astype(BF16)
        leave(2 * j + 1, pl.ds(j * half, half), grad, grad_hbm)
    for copy in copies:
        copy.wait()


def sum_all(flat):
    def trade(parts, axis, order):
        return lax.all_to_all(parts, axis, 0, 0, axis_index_groups=[order])

    part = trade(flat.reshape(32, 9, 1, 128), PLANE, PLANE_ORDER).sum(0)
    part = trade(jnp.broadcast_to(part[None], (16, 9, 1, 128)), "z", Z_ORDER).sum(0)
    whole = trade(jnp.broadcast_to(part[None], (32, 9, 1, 128)), PLANE, PLANE_ORDER)
    return whole.reshape(288, 128)


VMEM = pl.BlockSpec(memory_space=pltpu.VMEM)
HBM = pl.BlockSpec(memory_space=pltpu.HBM)
PARAMS = pltpu.CompilerParams(vmem_limit_bytes=32 * 1024 * 1024)


def per_device(
    points,
    counts,
    norm_gain,
    w_fx,
    w_slice,
    temper,
    query_projection,
    key_projection,
    value_projection,
    w_out,
    cotangent,
):
    rows, width = points.shape
    gain = norm_gain.reshape(1, width)
    n = HEADS * SLICES
    kept = (points, gain, w_slice, w_fx, w_out, cotangent)
    projections = (query_projection, key_projection, value_projection)

    def like(*shapes):
        return tuple(jax.ShapeDtypeStruct(shape, kind) for shape, kind in shapes)

    flat, whole, w_bf, c_t, scales, w_hi, w_lo, *kept = pl.pallas_call(
        front_kernel,
        out_shape=like(
            ((288, 128), F32),
            ((HEADS, rows), F32),
            ((n, rows), BF16),
            ((n, rows), BF16),
            ((HEADS, rows), F32),
            ((n, 384), BF16),
            ((n, 384), BF16),
            *((a.shape, a.dtype) for a in kept),
        ),
        in_specs=[VMEM] + [HBM] * 10,
        out_specs=(VMEM,) * 13,
        scratch_shapes=[
            *(pltpu.VMEM(a.shape, F32) for a in projections),
            pltpu.SMEM((HEADS,), F32),
            pltpu.VMEM((n, rows), F32),
            pltpu.SemaphoreType.DMA((10,)),
        ],
        compiler_params=PARAMS,
        name="front",
    )(
        counts,
        *(pltpu.with_memory_space_constraint(a, pltpu.HBM) for a in (temper, *kept, *projections)),
    )
    return pl.pallas_call(
        back_kernel,
        out_shape=like(((rows, width), BF16), ((rows, width), BF16)),
        in_specs=[VMEM] * 13,
        out_specs=(HBM,) * 2,
        scratch_shapes=[
            pltpu.VMEM((rows, width), BF16),
            pltpu.VMEM((rows, width), BF16),
            pltpu.VMEM((n, rows), BF16),
            pltpu.VMEM((width, rows), BF16),
            pltpu.VMEM((width, rows), F32),
            pltpu.SemaphoreType.DMA((4,)),
        ],
        compiler_params=PARAMS,
        name="back",
    )(sum_all(flat), whole, w_bf, c_t, scales, *kept, w_hi, w_lo)


def solution(mesh):
    fine = Mesh(mesh.devices.reshape(16, 2, 2, 2, 4), ALL)
    rows = P(ALL, None)
    return jax.shard_map(
        per_device,
        mesh=fine,
        in_specs=(rows, P(("z", "xh", "c"), ("xl", "y"))) + (P(),) * 8 + (rows,),
        out_specs=(rows, rows),
        check_vma=False,
    )
```

```python
import math

import jax
import jax.numpy as jnp
from jax import lax
from jax.experimental import pallas as pl
from jax.experimental.pallas import tpu as pltpu
from jax.sharding import Mesh, PartitionSpec as P

PLANE = ("xh", "c", "xl", "y")
ALL = ("z", "xh", "c", "xl", "y")
HEADS, SLICES, DH = 8, 64, 32
Z_ORDER = [9, 8, 10, 7, 11, 6, 12, 5, 13, 4, 14, 3, 15, 2, 1, 0]
PLANE_ORDER = [26, 18, *(i for i in range(32) if i not in (26, 18, 8)), 8]
F32, BF16 = jnp.float32, jnp.bfloat16


def dot(a, b, ca, cb, precision=None):
    return lax.dot_general(
        a, b, (((ca,), (cb,)), ((), ())), precision=precision, preferred_element_type=F32
    )


def parts(a):
    hi = a.astype(BF16)
    return hi, (a - hi.astype(F32)).astype(BF16)


def dot3(a, b, ca, cb):
    n = b[0].shape[1 - cb]
    left = jnp.concatenate(a, ca)
    right = jnp.concatenate([jnp.concatenate([b[0], b[0]], cb), jnp.concatenate([b[1], jnp.zeros_like(b[1])], cb)], 1 - cb)
    both = dot(left, right, ca, cb)
    return both[:, :n] + both[:, n:]


def normalise(x):
    cent = x - jnp.mean(x, -1, keepdims=True)
    rstd = lax.rsqrt(jnp.mean(cent * cent, -1, keepdims=True) + 1e-05)
    return cent * rstd, rstd


def front_kernel(*refs):
    count, temper_hbm = refs[:2]
    sources = refs[2:11]
    flat, whole, w_bf, c_t, scales, w_hi, w_lo = refs[11:18]
    temper, logit_t, sems = refs[27:30]
    targets = refs[18:24] + refs[24:27]
    x_ref, gain, w_slice, w_fx, w_out, cot = targets[:6]
    rows = x_ref.shape[0]
    copies = [
        pltpu.make_async_copy(a, b, sems.at[i])
        for i, (a, b) in enumerate(zip((*sources, temper_hbm), (*targets, temper)))
    ]
    for copy in copies:
        copy.start()
    copies[0].wait()
    copies[1].wait()
    normed = (normalise(x_ref[...].astype(F32))[0] * gain[...]).astype(BF16)
    for copy in copies[2:]:
        copy.wait()
    logit_t[...] = dot(w_slice[...].T, normed, 1, 1)
    stack_weights(*targets[6:], w_hi, w_lo)
    feats = dot(w_fx[...].T, normed, 1, 1).astype(BF16)
    gmix = dot(w_out[...], cot[...], 1, 1).astype(BF16)
    for h in range(HEADS):
        c_t[h * 64 : h * 64 + 32, :] = feats[h * 32 : h * 32 + 32, :]
        c_t[h * 64 + 32 : h * 64 + 64, :] = gmix[h * 32 : h * 32 + 32, :]
    live = (lax.broadcasted_iota(jnp.int32, (1, rows), 1) < count[...]).astype(F32)
    for h in range(HEADS):
        part = slice(h * SLICES, (h + 1) * SLICES)
        logits = logit_t[part, :]
        scale = 1.0 / jnp.full((1, rows), temper[h], F32)
        scales[h : h + 1, :] = scale
        e = jnp.exp((logits - jnp.max(logits, 0, keepdims=True)) * scale)
        w = e * (live / jnp.sum(e, 0, keepdims=True))
        w = w.astype(BF16)
        w_bf[part, :] = w
        whole[h : h + 1, :] = 1.0 / jnp.maximum(jnp.sum(w.astype(F32), 0, keepdims=True), 0.5)
    lane = lax.broadcasted_iota(jnp.int32, (64, 128), 1)
    for p in range(4):
        part = slice(p * 128, (p + 1) * 128)
        both = dot(w_bf[part, :], c_t[part, :], 1, 1)
        flat[p * 64 : (p + 1) * 64, :] = jnp.where(lane < 64, both[:64], both[64:])
    den = jnp.sum(w_bf[...].astype(F32), 1, keepdims=True)
    den = jnp.broadcast_to(den, (den.shape[0], 128)).T
    flat[256:288, :] = jnp.zeros((32, 128), F32)
    for p in range(4):
        flat[256 + p : 257 + p, :] = den[0:1, p * 128 : (p + 1) * 128]


def stack_weights(query, key, value, hi, lo):
    for h in range(HEADS):
        q, k, v = query[h], key[h], value[h]
        a, a_t, v_t = dot3(parts(q), parts(k), 1, 1), dot3(parts(k), parts(q), 1, 1), v.T
        none, gap = jnp.zeros((32, 32), F32), jnp.zeros((32, 64), F32)

        def at(left, right):
            block = jnp.concatenate([left, right], 1)
            return [block, gap] if h % 2 == 0 else [gap, block]

        upper = jnp.concatenate([*at(a, v), *at(a_t, none), gap, gap], 1)
        lower = jnp.concatenate([gap, gap, gap, gap, *at(v_t, none)], 1)
        whole = jnp.concatenate([upper, lower], 0)
        for ref, part in zip((hi, lo), parts(whole)):
            ref[h * 64 : (h + 1) * 64, :] = part


def middle(flat, w_hi, w_lo):
    row = lax.broadcasted_iota(jnp.int32, (128, 128), 0)
    lane = lax.broadcasted_iota(jnp.int32, (128, 128), 1)
    own = row // 64 == lane // 64
    second = (lane // 32) % 2 == 1
    scale = 1.0 / math.sqrt(DH)
    pairs = range(4)

    def each(f, *lists):
        return [f(*items) for items in zip(*lists)]

    def part(p):
        return slice(p * 128, (p + 1) * 128)

    t = [flat[p * 64 : (p + 1) * 64, :] for p in pairs]
    t = each(lambda t: jnp.where(own, jnp.concatenate([t, t], 0), 0.0), t)
    num = each(lambda t: jnp.where(second, 0.0, t), t)
    rec = 1.0 / (flat[256:264, :] + 1e-05)
    along = [rec[p : p + 1, :] for p in pairs]
    rec = rec.T
    down = [rec[:, p : p + 1] for p in pairs]
    split = each(parts, t)
    raw = [dot3(split[p], (w_hi[part(p), :], w_lo[part(p), :]), 1, 0) for p in pairs]
    u_v, u_t, g_v = (each(lambda a: parts(a[:, part(i)]), raw) for i in range(3))
    num_split = each(parts, num)
    s = each(
        lambda u, n, a, d: jnp.where(own, dot3(u, n, 1, 1) * (scale * a) * d, -jnp.inf),
        u_v, num_split, along, down,
    )
    g_prob = each(lambda g, n, a: dot3(g, n, 1, 1) * a, g_v, num_split, along)
    e = each(lambda s: jnp.exp(s - jnp.max(s, -1, keepdims=True)), s)
    prob = each(lambda e: e * (1.0 / jnp.sum(e, -1, keepdims=True)), e)
    g_s = each(lambda w, g: w * (g - jnp.sum(w * g, -1, keepdims=True)) * scale, prob, g_prob)
    g_tok = each(
        lambda g, w, u_v, u_t, g_v, a, d: dot3(parts(g * a), u_t, 1, 0)
        + dot3(parts(g * d), u_v, 0, 0)
        + dot3(parts(w), g_v, 0, 0),
        g_s, prob, u_v, u_t, g_v, along, down,
    )
    att = each(lambda w, a, v: dot3(parts(w * a), v, 1, 0), prob, along, u_v)
    blocks = each(lambda a, g, d: jnp.where(second, a, g * d), att, g_tok, down)
    g_den = each(lambda n, b, d: -jnp.sum(n * b, -1, keepdims=True) * d, num, blocks, down)
    return blocks, g_den


def back_kernel(
    flat, whole, w_bf, c_t, scales, x_ref, gain, w_slice, w_fx, w_out, cot, w_hi, w_lo,
    updated_hbm, grad_hbm, updated, grad, g_logit, g_feat, mixed_t, sems,
):
    hats = [normalise(x_ref[j * 256 : (j + 1) * 256, :].astype(F32)) for j in range(2)]
    blocks, g_den = middle(flat, w_hi, w_lo)
    split = [parts(b) for b in blocks]
    total, width = x_ref.shape
    half = total // 2
    copies = []

    def leave(i, at, source, target):
        copies.append(pltpu.make_async_copy(source.at[at], target.at[at], sems.at[i]))
        copies[-1].start()

    for j in range(2):
        at = slice(j * half, (j + 1) * half)
        for p in range(4):
            part = slice(p * 128, (p + 1) * 128)
            c = c_t[part, at]
            g_w = dot(jnp.concatenate(split[p], 1), jnp.concatenate([c, c], 0), 1, 0) + g_den[p]
            both = dot(split[p][0], w_bf[part, at], 0, 0)
            for i in range(2):
                h = 2 * p + i
                mine = slice(h * SLICES, (h + 1) * SLICES)
                w, g = w_bf[mine, at].astype(F32), g_w[i * 64 : (i + 1) * 64]
                mean = jnp.sum(w * g, 0, keepdims=True) * whole[h : h + 1, at]
                g_logit[mine, at] = (w * (g - mean) * scales[h : h + 1, at]).astype(BF16)
                g_feat[h * 32 : (h + 1) * 32, at] = both[i * 64 : i * 64 + 32].astype(BF16)
                mixed_t[h * 32 : (h + 1) * 32, at] = both[i * 64 + 32 : i * 64 + 64]
        x = x_ref[at, :].astype(F32)
        mixed = mixed_t[:, at].T.astype(BF16)
        updated[at, :] = (x + dot(mixed, w_out[...], 1, 0)).astype(BF16)
        leave(2 * j, pl.ds(j * half, half), updated, updated_hbm)
        g_normed = dot(w_slice[...], g_logit[:, at], 1, 0) + dot(w_fx[...], g_feat[:, at], 1, 0)
        g_normed = g_normed.T.astype(BF16).astype(F32)
        hat, rstd = hats[j]
        g_hat = g_normed * gain[...]
        along = jnp.mean(g_hat * hat, -1, keepdims=True)
        g_x = rstd * (g_hat - jnp.mean(g_hat, -1, keepdims=True) - hat * along)
        grad[at, :] = (cot[at, :].astype(F32) + g_x).astype(BF16)
        leave(2 * j + 1, pl.ds(j * half, half), grad, grad_hbm)
    for copy in copies:
        copy.wait()


def sum_all(flat):
    def trade(parts, axis, order):
        return lax.all_to_all(parts, axis, 0, 0, axis_index_groups=[order])

    part = trade(flat.reshape(32, 9, 1, 128), PLANE, PLANE_ORDER).sum(0)
    part = trade(jnp.broadcast_to(part[None], (16, 9, 1, 128)), "z", Z_ORDER).sum(0)
    whole = trade(jnp.broadcast_to(part[None], (32, 9, 1, 128)), PLANE, PLANE_ORDER)
    return whole.reshape(288, 128)


VMEM = pl.BlockSpec(memory_space=pltpu.VMEM)
HBM = pl.BlockSpec(memory_space=pltpu.HBM)
PARAMS = pltpu.CompilerParams(vmem_limit_bytes=32 * 1024 * 1024)


def per_device(
    points,
    counts,
    norm_gain,
    w_fx,
    w_slice,
    temper,
    query_projection,
    key_projection,
    value_projection,
    w_out,
    cotangent,
):
    rows, width = points.shape
    gain = norm_gain.reshape(1, width)
    n = HEADS * SLICES
    kept = (points, gain, w_slice, w_fx, w_out, cotangent)
    projections = (query_projection, key_projection, value_projection)

    def like(*shapes):
        return tuple(jax.ShapeDtypeStruct(shape, kind) for shape, kind in shapes)

    flat, whole, w_bf, c_t, scales, w_hi, w_lo, *kept = pl.pallas_call(
        front_kernel,
        out_shape=like(
            ((288, 128), F32),
            ((HEADS, rows), F32),
            ((n, rows), BF16),
            ((n, rows), BF16),
            ((HEADS, rows), F32),
            ((n, 384), BF16),
            ((n, 384), BF16),
            *((a.shape, a.dtype) for a in kept),
        ),
        in_specs=[VMEM] + [HBM] * 10,
        out_specs=(VMEM,) * 13,
        scratch_shapes=[
            *(pltpu.VMEM(a.shape, F32) for a in projections),
            pltpu.SMEM((HEADS,), F32),
            pltpu.VMEM((n, rows), F32),
            pltpu.SemaphoreType.DMA((10,)),
        ],
        compiler_params=PARAMS,
        name="front",
    )(
        counts,
        *(pltpu.with_memory_space_constraint(a, pltpu.HBM) for a in (temper, *kept, *projections)),
    )
    return pl.pallas_call(
        back_kernel,
        out_shape=like(((rows, width), BF16), ((rows, width), BF16)),
        in_specs=[VMEM] * 13,
        out_specs=(HBM,) * 2,
        scratch_shapes=[
            pltpu.VMEM((rows, width), BF16),
            pltpu.VMEM((rows, width), BF16),
            pltpu.VMEM((n, rows), BF16),
            pltpu.VMEM((width, rows), BF16),
            pltpu.VMEM((width, rows), F32),
            pltpu.SemaphoreType.DMA((4,)),
        ],
        compiler_params=PARAMS,
        name="back",
    )(sum_all(flat), whole, w_bf, c_t, scales, *kept, w_hi, w_lo)


def solution(mesh):
    fine = Mesh(mesh.devices.reshape(16, 2, 2, 2, 4), ALL)
    rows = P(ALL, None)
    return jax.shard_map(
        per_device,
        mesh=fine,
        in_specs=(rows, P(("z", "xh", "c"), ("xl", "y"))) + (P(),) * 8 + (rows,),
        out_specs=(rows, rows),
        check_vma=False,
    )
```
